32 devices in a mesh: gx: 4 (over y, x), gy: 8 (over z, core).
Axes of the slice: x: 2, y: 2, z: 4, core: 2. Of those that a mesh axis runs over, the one named last changes fastest.
Arguments:
- patches: bfloat16 [512, 6144], P('gy', 'gx'), may hold values from -2000 to 2000
- norm_gain: float32 [6144], P('gx'), may hold values from 0.5 to 1.5
- w_up: bfloat16 [6144, 24576], P('gx', 'gy'), may hold values from -0.078125 to 0.078125
- bias_up: float32 [24576], P('gy'), may hold values from -4 to 4
- w_down: bfloat16 [24576, 6144], P('gy', 'gx'), may hold values from -0.0390625 to 0.0390625
- bias_down: float32 [6144], P('gx'), may hold values from -4 to 4
- cotangent: bfloat16 [512, 6144], P('gy', 'gx'), may hold values from -4 to 4
Outputs:
- mlp_out: bfloat16 [512, 6144], P('gy', 'gx')
- grad_patches: bfloat16 [512, 6144], P('gy', 'gx')
- grad_gain: float32 [6144], P('gx')
- grad_w_up: float32 [6144, 24576], P('gx', 'gy')
- grad_bias_up: float32 [24576], P('gy')
- grad_w_down: float32 [24576, 6144], P('gy', 'gx')
- grad_bias_down: float32 [6144], P('gx')
The draws below stay inside these ranges and needn't reach their ends.
All inputs are finite; a program needn't handle non-finite values.
Results may differ from the reference program's by a relative error of at most 0.007.
Values may be sent and summed in bfloat16 or wider, within the bound.
No kernel may reach another device: no remote copies, remote signals or barrier semaphores. Data moves between devices by JAX's collectives and lax.ppermute only.
A program may use at most 128 MiB of HBM per device.

```python
import jax
import jax.numpy as jnp
from jax import lax

D = 6144
FF = 24576
TOKENS = 512


def draw_patches(key, part):
    keys = jax.random.split(key, 4)
    rising = jnp.exp(jnp.log(3.0) * jnp.arange(D, dtype=jnp.float32) / D)
    column_scale = rising * jnp.exp(jax.random.uniform(keys[0], (D,), jnp.float32, 0.0, jnp.log(10.0)))
    row_scale = jnp.exp(jax.random.uniform(keys[1], (TOKENS, 1), jnp.float32, 0.0, jnp.log(10.0)))
    noise = jnp.clip(jax.random.normal(keys[2], (TOKENS, D), jnp.float32), -5.0, 5.0)
    offset = jnp.clip(0.3 * jax.random.normal(keys[3], (D,), jnp.float32), -1.0, 1.0)
    return (row_scale * column_scale * (noise + offset)).astype(jnp.bfloat16)


def block_levels(rng, extent, shards, least, largest):
    loudness = 1.0
    for axis_at, shards_of in shards:
        heights = jax.random.uniform(jax.random.fold_in(jax.random.fold_in(rng, 6), axis_at), (shards_of,), jnp.float32, least / len(shards), largest / len(shards))
        loudness = loudness * jnp.repeat(jnp.exp(heights), extent[axis_at] // shards_of).reshape((-1,) + (1,) * (len(extent) - 1 - axis_at))
    return loudness


def centred(stream_key, dims, width, reach, cuts=(), held_as=jnp.bfloat16):
    factor_of = block_levels(stream_key, dims, cuts, -0.22, 0.18) if cuts else 1.0
    values = jax.random.normal(stream_key, dims, jnp.float32) * width * factor_of
    return jnp.minimum(jnp.maximum(values, -reach), reach).astype(held_as)


def setup_inputs(seed: int = 0) -> dict:
    splits = jax.random.split(jax.random.key(seed), 8)
    return {
        "patches": draw_patches(jax.random.fold_in(splits[7], 71), 0),
        "norm_gain": jnp.clip(0.5 + 1.0 * jax.random.uniform(splits[1], (D,), jnp.float32) ** block_levels(splits[1], (D,), ((0, 4),), -0.2, 0.2), 0.5, 1.5),
        "w_up": centred(splits[2], (D, FF), D ** -0.5, 0.078125, ((0, 4), (1, 8))),
        "bias_up": centred(splits[3], (FF,), 1.0, 4.0, ((0, 8),), jnp.float32),
        "w_down": centred(splits[4], (FF, D), FF ** -0.5, 0.0390625, ((0, 8), (1, 4))),
        "bias_down": centred(splits[5], (D,), 1.0, 4.0, ((0, 4),), jnp.float32),
        "cotangent": centred(splits[6], (TOKENS, D), 0.5, 4.0, ((0, 8), (1, 4))),
    }


epsilon = 1e-06
inv_root_two = 0.7071067811865476
inv_root_two_pi = 0.3989422804014327

def gelu_value(hidden):
    return 0.5 * hidden * (1.0 + lax.erf(hidden * inv_root_two))

def gelu_slope(hidden):
    return 0.5 * (1.0 + lax.erf(hidden * inv_root_two)) + hidden * jnp.exp(-0.5 * hidden * hidden) * inv_root_two_pi

def reference(patches, norm_gain, w_up, bias_up, w_down, bias_down, cotangent):
    values = patches.astype(jnp.float32)
    row_mean = lax.optimization_barrier(jnp.sum(values, axis=1, keepdims=True)) / D
    variance = lax.optimization_barrier(jnp.sum(values * values, axis=1, keepdims=True)) / D - row_mean * row_mean
    inv_std = lax.rsqrt(variance + epsilon)
    standard = (values - row_mean) * inv_std
    normed = (standard * norm_gain).astype(jnp.bfloat16)
    hidden = jnp.dot(normed, w_up, preferred_element_type=jnp.float32) + bias_up
    activated = gelu_value(hidden).astype(jnp.bfloat16)
    mlp_out = (jnp.dot(activated, w_down, preferred_element_type=jnp.float32) + bias_down).astype(jnp.bfloat16)
    grad_bias_down = lax.optimization_barrier(jnp.sum(cotangent.astype(jnp.float32), axis=0))
    grad_w_down = jnp.dot(activated.T, cotangent, preferred_element_type=jnp.float32)
    grad_act = jnp.dot(cotangent, w_down.T, preferred_element_type=jnp.float32)
    grad_hidden = (grad_act * gelu_slope(hidden)).astype(jnp.bfloat16)
    grad_bias_up = lax.optimization_barrier(jnp.sum(grad_hidden.astype(jnp.float32), axis=0))
    grad_w_up = jnp.dot(normed.T, grad_hidden, preferred_element_type=jnp.float32)
    grad_normed = jnp.dot(grad_hidden, w_up.T, preferred_element_type=jnp.float32)
    grad_gain = lax.optimization_barrier(jnp.sum(grad_normed * standard, axis=0))
    scaled = grad_normed * norm_gain
    first_mean = lax.optimization_barrier(jnp.sum(scaled, axis=1, keepdims=True)) / D
    second_mean = lax.optimization_barrier(jnp.sum(scaled * standard, axis=1, keepdims=True)) / D
    grad_patches = (inv_std * (scaled - first_mean - standard * second_mean)).astype(jnp.bfloat16)
    return (mlp_out, grad_patches, grad_gain, grad_w_up, grad_bias_up, grad_w_down, grad_bias_down)
```

```python
import jax
import jax.numpy as jnp
from jax import lax
from jax.experimental import pallas as pl
from jax.experimental.pallas import tpu as pltpu
from jax.sharding import PartitionSpec as P

D = 6144

epsilon = 1e-06
inv_root_two = 0.7071067811865476
inv_root_two_pi = 0.3989422804014327

bf16 = jnp.bfloat16
f32 = jnp.float32
VMEM_LIMIT = 40 * 1024 * 1024

NN = (((1,), (0,)), ((), ()))
NT = (((1,), (1,)), ((), ()))
TN = (((0,), (0,)), ((), ()))


def mm(left, right, dims):
    return lax.dot_general(left, right, dims, preferred_element_type=f32)


def cost(m, k, n, moved):
    return pl.CostEstimate(flops=2 * m * k * n, bytes_accessed=moved, transcendentals=0)


def params():
    return pltpu.CompilerParams(vmem_limit_bytes=VMEM_LIMIT)


def block_of(width, most=384):
    return most if width % most == 0 else width


def bits(n):
    return [1 << b for b in range(n.bit_length() - 1)]


def partial_product(x, w, me, shard, rels, dtype, by_rows):
    rows, depth = x.shape
    nb = block_of(shard)
    per = shard // nb
    steps = per * len(rels)
    index = jnp.concatenate([(me ^ r) * per + jnp.arange(per, dtype=jnp.int32) for r in rels])

    def kernel(index_ref, x_ref, w_ref, o_ref):
        o_ref[...] = mm(x_ref[...], w_ref[...], NT if by_rows else NN).astype(dtype)

    if by_rows:
        w_spec = pl.BlockSpec((nb, depth), lambda j, at: (at[j], 0))
    else:
        w_spec = pl.BlockSpec((depth, nb), lambda j, at: (0, at[j]))
    n = steps * nb
    return pl.pallas_call(
        kernel,
        grid_spec=pltpu.PrefetchScalarGridSpec(
            num_scalar_prefetch=1,
            grid=(steps,),
            in_specs=[pl.BlockSpec((rows, depth), lambda j, at: (0, 0)), w_spec],
            out_specs=pl.BlockSpec((rows, nb), lambda j, at: (0, j)),
        ),
        out_shape=jax.ShapeDtypeStruct((rows, n), dtype),
        compiler_params=params(),
        cost_estimate=cost(rows, depth, n, 2 * rows * depth + 2 * depth * n + 4 * rows * n),
    )(index, x, w)


def summed_product(near, far, w, me, by_rows):
    rows, wide = near.shape
    shard = wide // 2
    out = w.shape[1] if by_rows else w.shape[0]
    nb = 256
    half = rows // 2

    def kernel(me_ref, near_ref, far_ref, w0, w2, w1, w3, keep_ref, go_ref):
        dims = NN if by_rows else NT
        total = mm(near_ref[:, :shard], w0[...], dims)
        total += mm(near_ref[:, shard:], w2[...], dims)
        total += mm(far_ref[:, :shard], w1[...], dims)
        total += mm(far_ref[:, shard:], w3[...], dims)
        keep_ref[...] = total[:half]
        go_ref[...] = total[half:].astype(bf16)

    def w_spec(r):
        if by_rows:
            return pl.BlockSpec((shard, nb), lambda j, at: (at[0] ^ r, j))
        return pl.BlockSpec((nb, shard), lambda j, at: (j, at[0] ^ r))

    whole = pl.BlockSpec((rows, wide), lambda j, at: (0, 0))
    return pl.pallas_call(
        kernel,
        grid_spec=pltpu.PrefetchScalarGridSpec(
            num_scalar_prefetch=1,
            grid=(out // nb,),
            in_specs=[whole, whole, w_spec(0), w_spec(2), w_spec(1), w_spec(3)],
            out_specs=[pl.BlockSpec((half, nb), lambda j, at: (0, j))] * 2,
        ),
        out_shape=(jax.ShapeDtypeStruct((half, out), f32), jax.ShapeDtypeStruct((half, out), bf16)),
        compiler_params=params(),
        cost_estimate=cost(rows, 2 * wide, out, 4 * rows * wide + 4 * wide * out + 3 * rows * out),
    )(me.reshape(1), near, far, w, w, w, w)


def weight_grad_down(pieces, cots, me, rels, shard, units, so_far):
    nb = block_of(shard)
    per = shard // nb
    out = cots[0].shape[1]
    tokens = sum(c.shape[0] for c in cots)
    index = jnp.concatenate([(me ^ r) * per + jnp.arange(per, dtype=jnp.int32) for r in rels])

    def kernel(index_ref, p0, p1, c0, c1, *refs):
        refs[-1][...] = mm(p0[...], c0[...], TN) + mm(p1[...], c1[...], TN)

    in_specs = [pl.BlockSpec((p.shape[0], nb), lambda j, at: (0, j)) for p in pieces]
    in_specs += [pl.BlockSpec(c.shape, lambda j, at: (0, 0)) for c in cots]
    rest = ()
    if so_far is not None:
        in_specs.append(pl.BlockSpec(memory_space=pl.ANY))
        rest = (so_far,)
    return pl.pallas_call(
        kernel,
        grid_spec=pltpu.PrefetchScalarGridSpec(
            num_scalar_prefetch=1,
            grid=(per * len(rels),),
            in_specs=in_specs,
            out_specs=pl.BlockSpec((nb, out), lambda j, at: (at[j], 0)),
        ),
        out_shape=jax.ShapeDtypeStruct((units, out), f32),
        input_output_aliases={5: 0} if rest else {},
        compiler_params=params(),
        cost_estimate=cost(shard * len(rels), tokens, out, 4 * shard * len(rels) * out),
    )(index, *pieces, *cots, *rest)


def weight_grad_up(normeds, pieces, me, rels, shard, units, so_far):
    nb = block_of(shard)
    per = shard // nb
    out = normeds[0].shape[1]
    tokens = sum(c.shape[0] for c in normeds)
    index = jnp.concatenate([(me ^ r) * per + jnp.arange(per, dtype=jnp.int32) for r in rels])

    def kernel(index_ref, n0, n1, p0, p1, *refs):
        refs[-2][...] = mm(n0[...], p0[...], TN) + mm(n1[...], p1[...], TN)
        refs[-1][...] = jnp.sum(p0[...].astype(f32), axis=0, keepdims=True) + jnp.sum(
            p1[...].astype(f32), axis=0, keepdims=True
        )

    in_specs = [pl.BlockSpec(c.shape, lambda j, at: (0, 0)) for c in normeds]
    in_specs += [pl.BlockSpec((p.shape[0], nb), lambda j, at: (0, j)) for p in pieces]
    rest = ()
    if so_far is not None:
        in_specs += [pl.BlockSpec(memory_space=pl.ANY)] * 2
        rest = so_far
    return pl.pallas_call(
        kernel,
        grid_spec=pltpu.PrefetchScalarGridSpec(
            num_scalar_prefetch=1,
            grid=(per * len(rels),),
            in_specs=in_specs,
            out_specs=[
                pl.BlockSpec((out, nb), lambda j, at: (0, at[j])),
                pl.BlockSpec((1, nb), lambda j, at: (0, at[j])),
            ],
        ),
        out_shape=(jax.ShapeDtypeStruct((out, units), f32), jax.ShapeDtypeStruct((1, units), f32)),
        input_output_aliases={5: 0, 6: 1} if rest else {},
        compiler_params=params(),
        cost_estimate=cost(shard * len(rels), tokens, out, 4 * shard * len(rels) * out),
    )(index, *normeds, *pieces, *rest)


def solution(mesh):
    n_gx, n_gy = mesh.shape["gx"], mesh.shape["gy"]
    both = ("gx", "gy")

    def across(first):
        pairs = []
        for gx in range(n_gx):
            for gy in range(n_gy):
                flip = 1 if (gy % 2 == 0) == first else 2
                pairs.append((gx * n_gy + gy, (gx ^ flip) * n_gy + gy))
        return pairs

    first_pairs, second_pairs = across(True), across(False)

    def to_first(x):
        return lax.ppermute(x, both, first_pairs)

    def to_second(x):
        return lax.ppermute(x, both, second_pairs)

    def along_gy(x, m):
        return lax.ppermute(x, "gy", [(i, i ^ m) for i in range(n_gy)])

    def along_gx(x, m):
        return lax.ppermute(x, "gx", [(i, i ^ m) for i in range(n_gx)])

    def plane_sum(x):
        for step in bits(n_gx):
            x = x + along_gx(x, step)
        return x

    def gather_rows(own):
        near = jnp.concatenate([own, along_gy(own, 1)])
        even = jnp.concatenate([along_gy(own, 2 * k) for k in range(1, n_gy // 2)])
        return near, jnp.concatenate([even, along_gy(even, 1)])

    def scatter_plane(x, w, me, shard, by_rows):
        go = to_first(partial_product(x, w, me, shard, (2, 3), bf16, by_rows))
        keep = partial_product(x, w, me, shard, (0, 1), f32, by_rows)
        back = to_second((keep[:, shard:] + go[:, shard:].astype(f32)).astype(bf16))
        total = keep[:, :shard] + go[:, :shard].astype(f32) + back.astype(f32)
        for step in bits(n_gx)[2:]:
            total = total + along_gx(total, step)
        return total

    def gather_plane(x):
        near = jnp.concatenate([x, to_first(x)], axis=1)
        return near, to_second(near)

    def shards(patches, norm_gain, w_up, bias_up, w_down, bias_down, cotangent):
        rows = patches.shape[0]
        units = w_up.shape[1]
        shard = units // 4
        gx, gy = lax.axis_index("gx") % 4, lax.axis_index("gy")
        me = jnp.where(gy % 2 == 0, 2 * (gx % 2) + gx // 2, gx).astype(jnp.int32)

        cot = gather_rows(cotangent)
        values = patches.astype(f32)
        totals = plane_sum(jnp.stack([jnp.sum(values, axis=1), jnp.sum(values * values, axis=1)]))
        row_mean = (totals[0] / D)[:, None]
        variance = (totals[1] / D)[:, None] - row_mean * row_mean
        inv_std = lax.rsqrt(variance + epsilon)
        standard = (values - row_mean) * inv_std
        normed = gather_rows((standard * norm_gain).astype(bf16))

        bias = lax.dynamic_slice_in_dim(bias_up, me * shard, shard)

        def middle(c):
            grad_act = scatter_plane(cot[c], w_down, me, shard, True)
            hidden = scatter_plane(normed[c], w_up, me, shard, False) + bias
            upper = 0.5 * (1.0 + lax.erf(hidden * inv_root_two))
            act = (hidden * upper).astype(bf16)
            slope = upper + hidden * jnp.exp(-0.5 * hidden * hidden) * inv_root_two_pi
            return act, (grad_act * slope).astype(bf16)

        acts, grads = zip(*[middle(c) for c in range(2)])

        def send_home(keep, go):
            ready = (keep + along_gy(go, 1).astype(f32)).astype(bf16)
            return sum(
                along_gy(ready[(k - 1) * rows : k * rows], 2 * k).astype(f32) for k in range(1, n_gy // 2)
            )

        def at_home(keep, go):
            return keep + along_gy(go, 1).astype(f32)

        grad = [gather_plane(grads[c]) for c in range(2)]
        grad_normed = send_home(*summed_product(*grad[1], w_up, me, False))
        grad_normed += at_home(*summed_product(*grad[0], w_up, me, False))
        up = weight_grad_up(normed, (grad[0][0], grad[1][0]), me, (0, 2), shard, units, None)
        up = weight_grad_up(normed, (grad[0][1], grad[1][1]), me, (1, 3), shard, units, up)
        grad_w_up, grad_bias_up = up[0], up[1][0]

        act = [None, gather_plane(acts[1])]
        act[0] = gather_plane(acts[0])
        mlp_out = send_home(*summed_product(*act[1], w_down, me, True))
        mlp_out += at_home(*summed_product(*act[0], w_down, me, True))
        mlp_out = (mlp_out + bias_down).astype(bf16)
        down = weight_grad_down((act[0][0], act[1][0]), cot, me, (0, 2), shard, units, None)
        grad_w_down = weight_grad_down((act[0][1], act[1][1]), cot, me, (1, 3), shard, units, down)

        grad_bias_down = jnp.sum(cot[0].astype(f32), axis=0) + jnp.sum(cot[1].astype(f32), axis=0)

        grad_gain = jnp.sum(grad_normed * standard, axis=0)
        for step in bits(n_gy):
            grad_gain = grad_gain + along_gy(grad_gain, step)
        scaled = grad_normed * norm_gain
        sums = plane_sum(jnp.stack([jnp.sum(scaled, axis=1), jnp.sum(scaled * standard, axis=1)]))
        first_mean = (sums[0] / D)[:, None]
        second_mean = (sums[1] / D)[:, None]
        grad_patches = (inv_std * (scaled - first_mean - standard * second_mean)).astype(bf16)
        return mlp_out, grad_patches, grad_gain, grad_w_up, grad_bias_up, grad_w_down, grad_bias_down

    in_specs = (
        P("gy", "gx"),
        P("gx"),
        P("gx", "gy"),
        P("gy"),
        P("gy", "gx"),
        P("gx"),
        P("gy", "gx"),
    )
    out_specs = (
        P("gy", "gx"),
        P("gy", "gx"),
        P("gx"),
        P("gx", "gy"),
        P("gy"),
        P("gy", "gx"),
        P("gx"),
    )
    return jax.shard_map(shards, mesh=mesh, in_specs=in_specs, out_specs=out_specs, check_vma=False)
```

```python
import jax
import jax.numpy as jnp
from jax import lax
from jax.experimental import pallas as pl
from jax.experimental.pallas import tpu as pltpu
from jax.sharding import PartitionSpec as P

D = 6144

epsilon = 1e-06
inv_root_two = 0.7071067811865476
inv_root_two_pi = 0.3989422804014327

bf16 = jnp.bfloat16
f32 = jnp.float32
VMEM_LIMIT = 16 * 1024 * 1024

NN = (((1,), (0,)), ((), ()))
NT = (((1,), (1,)), ((), ()))
TN = (((0,), (0,)), ((), ()))


def mm(left, right, dims):
    return lax.dot_general(left, right, dims, preferred_element_type=f32)


def call(kernel, name, out_shape, in_specs, out_specs, flops, moved, scratch=(), aliases=None):
    return pl.pallas_call(
        kernel,
        name=name,
        out_shape=out_shape,
        in_specs=in_specs,
        out_specs=out_specs,
        scratch_shapes=scratch,
        input_output_aliases=aliases or {},
        compiler_params=pltpu.CompilerParams(vmem_limit_bytes=VMEM_LIMIT),
        cost_estimate=pl.CostEstimate(flops=0, bytes_accessed=0, transcendentals=0),
    )


IN_VMEM = pl.BlockSpec(memory_space=pltpu.VMEM)
IN_SMEM = pl.BlockSpec(memory_space=pltpu.SMEM)
IN_HBM = pl.BlockSpec(memory_space=pltpu.HBM)


def bits(n):
    return [1 << b for b in range(n.bit_length() - 1)]


def after(x, *others):
    return lax.optimization_barrier((x, *others))[0]


def block_at(me, rel, size):
    return pl.ds(pl.multiple_of((me ^ rel) * size, size), size)


def pieces_of(x_refs):
    return jnp.concatenate([x[...] for x in x_refs], axis=0)


def load_and_multiply(name, xs, w, me, shard, by_rows):
    rows, depth = sum(x.shape[0] for x in xs), xs[0].shape[1]

    def kernel(me_ref, *refs):
        x_refs, (w_ref, go_ref, keep_ref, all_ref, held_ref, sem) = refs[: len(xs)], refs[len(xs) :]

        def view(ref, r):
            at = block_at(me_ref[0], r, shard)
            return ref.at[at, :] if by_rows else ref.at[:, at]

        order, parts = (2, 3, 0, 1), 4
        copies = {}
        for r in order:
            for p in range(parts):
                source, target = view(w_ref, r), view(held_ref, r)
                span = pl.ds(p * (source.shape[0] // parts), source.shape[0] // parts)
                copies[r, p] = pltpu.make_async_copy(source.at[span, :], target.at[span, :], sem.at[r, p])
                copies[r, p].start()
        all_ref[...] = pieces_of(x_refs)
        for r, o_ref in zip(order, (go_ref, go_ref, keep_ref, keep_ref)):
            for p in range(parts):
                copies[r, p].wait()
            part = mm(all_ref[...], view(held_ref, r)[...], NT if by_rows else NN)
            o_ref[:, (r % 2) * shard : (r % 2 + 1) * shard] = part.astype(o_ref.dtype)

    return call(
        kernel,
        name,
        (
            jax.ShapeDtypeStruct((rows, 2 * shard), bf16),
            jax.ShapeDtypeStruct((rows, 2 * shard), f32),
            jax.ShapeDtypeStruct((rows, depth), bf16),
            pltpu.VMEM(w.shape, w.dtype),
        ),
        [IN_SMEM] + [IN_VMEM] * len(xs) + [IN_HBM],
        [IN_VMEM] * 4,
        8 * rows * depth * shard,
        2 * w.size,
        scratch=[pltpu.SemaphoreType.DMA((4, 4))],
    )(me, *xs, w)


def multiply(name, xs, w, me, shard, rels, dtype, by_rows):
    rows, depth = sum(x.shape[0] for x in xs), xs[0].shape[1]
    whole = len(xs) > 1

    def kernel(me_ref, *refs):
        x_refs, (w_ref, o_ref) = refs[: len(xs)], refs[len(xs) : len(xs) + 2]
        x_ref = x_refs[0]
        if whole:
            x_ref = refs[-1]
            x_ref[...] = pieces_of(x_refs)
        for j, r in enumerate(rels):
            at = block_at(me_ref[0], r, shard)
            block = w_ref[at, :] if by_rows else w_ref[:, at]
            o_ref[:, j * shard : (j + 1) * shard] = mm(x_ref[...], block, NT if by_rows else NN).astype(dtype)

    out_shape = [jax.ShapeDtypeStruct((rows, shard * len(rels)), dtype)]
    if whole:
        out_shape.append(jax.ShapeDtypeStruct((rows, depth), bf16))
    return call(
        kernel,
        name,
        out_shape,
        [IN_SMEM] + [IN_VMEM] * (len(xs) + 1),
        [IN_VMEM] * len(out_shape),
        2 * rows * depth * shard * len(rels),
        4 * rows * shard * len(rels),
    )(me, *xs, w)


def summed(near, far, w_ref, me, shard, cols, by_rows):
    total = None
    for r, ref, start in ((0, near, 0), (2, near, shard), (1, far, 0), (3, far, shard)):
        at = block_at(me, r, shard)
        block = w_ref[at, cols] if by_rows else w_ref[cols, at]
        term = mm(ref[:, start : start + shard], block, NN if by_rows else NT)
        total = term if total is None else total + term
    return total


def down_product(name, near, far, w_down, me):
    rows, wide = near.shape
    out = w_down.shape[1]
    half, shard, nb = rows // 2, wide // 2, 256

    def kernel(me_ref, near_ref, far_ref, w_ref, keep_ref, go_ref):
        for c in range(0, out, nb):
            cols = slice(c, c + nb)
            total = summed(near_ref, far_ref, w_ref, me_ref[0], shard, cols, True)
            keep_ref[:, cols] = total[:half]
            go_ref[:, cols] = total[half:].astype(bf16)

    return call(
        kernel,
        name,
        (jax.ShapeDtypeStruct((half, out), f32), jax.ShapeDtypeStruct((half, out), bf16)),
        [IN_SMEM] + [IN_VMEM] * 3,
        [IN_VMEM] * 2,
        4 * rows * wide * out,
        4 * rows * wide + 3 * rows * out,
    )(me, near, far, w_down)


def normed_grad(name, near, far, w_up, normed, me):
    rows, wide = near.shape
    out = w_up.shape[0]
    half, shard, nb = rows // 2, wide // 2, 256

    def kernel(me_ref, near_ref, far_ref, w_ref, n_ref, keep_ref, go_ref, gain_ref):
        for c in range(0, out, nb):
            cols = slice(c, c + nb)
            total = summed(near_ref, far_ref, w_ref, me_ref[0], shard, cols, False)
            keep_ref[:, cols] = total[:half]
            go_ref[:, cols] = total[half:].astype(bf16)
            gain_ref[:, cols] = jnp.sum(total * n_ref[:, cols].astype(f32), axis=0, keepdims=True)

    return call(
        kernel,
        name,
        (
            jax.ShapeDtypeStruct((half, out), f32),
            jax.ShapeDtypeStruct((half, out), bf16),
            jax.ShapeDtypeStruct((1, out), f32),
        ),
        [IN_SMEM] + [IN_VMEM] * 4,
        [IN_VMEM] * 3,
        4 * rows * wide * out,
        4 * rows * wide + 3 * rows * out,
    )(me, near, far, w_up, normed)


def stream_out(steps, compute, place, buf, sem):
    copies = []
    for i in range(steps):
        if i >= 2:
            copies[i - 2].wait()
        buf[i % 2] = compute(i)
        copies.append(pltpu.make_async_copy(buf.at[i % 2], place(i), sem.at[i % 2]))
        copies[i].start()
    for c in copies[-2:]:
        c.wait()


def weight_grad_down(name, pieces, cots, me, rels, shard, units, so_far):
    nb = shard // 2
    out = cots[0].shape[1]
    tokens = sum(c.shape[0] for c in cots)
    steps = 2 * len(rels)

    def kernel(me_ref, p0, p1, c0, c1, *refs):
        o_ref, buf, sem = refs[-3:]

        def compute(i):
            cols = slice(i * nb, (i + 1) * nb)
            return mm(p0[:, cols], c0[...], TN) + mm(p1[:, cols], c1[...], TN)

        def place(i):
            start = (me_ref[0] ^ rels[i // 2]) * shard + (i % 2) * nb
            return o_ref.at[pl.ds(pl.multiple_of(start, nb), nb), :]

        stream_out(steps, compute, place, buf, sem)

    rest = () if so_far is None else (so_far,)
    return call(
        kernel,
        name,
        jax.ShapeDtypeStruct((units, out), f32),
        [IN_SMEM] + [IN_VMEM] * 4 + [IN_HBM] * len(rest),
        IN_HBM,
        2 * tokens * nb * steps * out,
        4 * nb * steps * out,
        scratch=[pltpu.VMEM((2, nb, out), f32), pltpu.SemaphoreType.DMA((2,))],
        aliases={5: 0} if rest else None,
    )(me, *pieces, *cots, *rest)


def weight_grad_up(normed, nears, fars, me, units):
    out = normed[0].shape[1]
    tokens = sum(n.shape[0] for n in nears)
    shard = nears[0].shape[1] // 2
    nb = 256
    steps = out // nb

    def kernel(me_ref, n0, n1, near0, near1, far0, far1, o_ref, sum_ref, buf, sem):
        four = ((0, near0, near1, 0), (2, near0, near1, shard), (1, far0, far1, 0), (3, far0, far1, shard))
        for r, p0, p1, start in four:
            at = slice(start, start + shard)
            total = jnp.sum(p0[:, at].astype(f32), axis=0, keepdims=True)
            total += jnp.sum(p1[:, at].astype(f32), axis=0, keepdims=True)
            sum_ref[:, block_at(me_ref[0], r, shard)] = total

        copies = []
        for i in range(steps):
            if i >= 2:
                copies[i - 2].wait()
            rows = slice(i * nb, (i + 1) * nb)
            t0, t1 = n0[:, rows].T, n1[:, rows].T
            for r, p0, p1, start in four:
                at = slice(start, start + shard)
                term = mm(t0, p0[:, at], NN) + mm(t1, p1[:, at], NN)
                buf[i % 2, :, block_at(me_ref[0], r, shard)] = term
            copies.append(pltpu.make_async_copy(buf.at[i % 2], o_ref.at[rows, :], sem.at[i % 2]))
            copies[i].start()
        for c in copies[-2:]:
            c.wait()

    return call(
        kernel,
        "weight_grad_up",
        (jax.ShapeDtypeStruct((out, units), f32), jax.ShapeDtypeStruct((1, units), f32)),
        [IN_SMEM] + [IN_VMEM] * 6,
        [IN_HBM, IN_VMEM],
        2 * tokens * units * out,
        4 * units * out,
        scratch=[pltpu.VMEM((2, nb, units), f32), pltpu.SemaphoreType.DMA((2,))],
    )(me, *normed, *nears, *fars)


def solution(mesh):
    n_gx, n_gy = mesh.shape["gx"], mesh.shape["gy"]
    both = ("gx", "gy")
    chips = n_gy // 2

    def across(first):
        pairs = []
        for gx in range(n_gx):
            for gy in range(n_gy):
                flip = 1 if (gy % 2 == 0) == first else 2
                pairs.append((gx * n_gy + gy, (gx ^ flip) * n_gy + gy))
        return pairs

    first_pairs, second_pairs = across(True), across(False)

    def to_first(x):
        return lax.ppermute(x, both, first_pairs)

    def to_second(x):
        return lax.ppermute(x, both, second_pairs)

    def along_gy(x, m):
        return lax.ppermute(x, "gy", [(i, i ^ m) for i in range(n_gy)])

    def along_gx(x, m):
        return lax.ppermute(x, "gx", [(i, i ^ m) for i in range(n_gx)])

    def plane_sum(x):
        for step in bits(n_gx):
            x = x + along_gx(x, step)
        return x

    def over_groups(total):
        for step in bits(n_gx)[2:]:
            total = total + along_gx(total, step)
        return total

    def for_second(keep, came, shard):
        return (keep[:, shard:] + came[:, shard:].astype(f32)).astype(bf16)

    def plane_total(keep, came, back, shard):
        return over_groups(keep[:, :shard] + came[:, :shard].astype(f32) + back.astype(f32))

    def shards(patches, norm_gain, w_up, bias_up, w_down, bias_down, cotangent):
        rows = patches.shape[0]
        units = w_up.shape[1]
        shard = units // 4
        gx, gy = lax.axis_index("gx") % 4, lax.axis_index("gy")
        me = jnp.where(gy % 2 == 0, 2 * (gx % 2) + gx // 2, gx).astype(jnp.int32)
        bias = lax.dynamic_slice_in_dim(bias_up, me * shard, shard)
        me = me.reshape(1)

        w_up = pltpu.with_memory_space_constraint(w_up, pltpu.HBM)
        w_down = pltpu.with_memory_space_constraint(w_down, pltpu.HBM)

        def gather(own):
            z1 = along_gy(own, 2)
            w = [own, z1, along_gy(own, 1), along_gy(z1, 1)]
            even = [own]
            for step in bits(chips)[1:]:
                even += [along_gy(e, 2 * step) for e in even]
            even = even[1:]
            even += [along_gy(e, 2) for e in even]
            even = jnp.concatenate(even)
            return w, [even, along_gy(even, 1)]

        cot_w, cot_x = gather(cotangent)
        values = patches.astype(f32)
        totals = plane_sum(jnp.stack([jnp.sum(values, axis=1), jnp.sum(values * values, axis=1)]))
        go, keep_gw, cot_w, w_down = load_and_multiply("grad_act_w", cot_w, w_down, me, shard, True)
        came_gw = to_first(go)
        totals = after(totals, go)

        row_mean = (totals[0] / D)[:, None]
        variance = (totals[1] / D)[:, None] - row_mean * row_mean
        inv_std = lax.rsqrt(variance + epsilon)
        standard = (values - row_mean) * inv_std
        normed_w, normed_x = gather((standard * norm_gain).astype(bf16))
        back_gw = to_second(for_second(keep_gw, came_gw, shard))
        go, cot_x = multiply("grad_act_x_go", cot_x, w_down, me, shard, (2, 3), bf16, True)
        came_gx = to_first(go)
        keep_gx = multiply("grad_act_x_keep", [cot_x], w_down, me, shard, (0, 1), f32, True)[0]
        normed_w[0] = after(normed_w[0], keep_gx)
        go, keep_hw, normed_w, w_up = load_and_multiply("hidden_w", normed_w, w_up, me, shard, False)
        came_hw = to_first(go)
        back_hw = to_second(for_second(keep_hw, came_hw, shard))
        back_gx = to_second(for_second(keep_gx, came_gx, shard))

        def middle(grad_act, hidden):
            hidden = hidden + bias
            upper = 0.5 * (1.0 + lax.erf(hidden * inv_root_two))
            act = (hidden * upper).astype(bf16)
            slope = upper + hidden * jnp.exp(-0.5 * hidden * hidden) * inv_root_two_pi
            return act, (grad_act * slope).astype(bf16)

        go, normed_x = multiply("hidden_x_go", normed_x, w_up, me, shard, (2, 3), bf16, False)
        came_hx = to_first(go)
        act_w, grad_w = middle(
            plane_total(keep_gw, came_gw, back_gw, shard), plane_total(keep_hw, came_hw, back_hw, shard)
        )
        keep_hx = multiply(
            "hidden_x_keep", [after(normed_x, act_w, grad_w)], w_up, me, shard, (0, 1), f32, False
        )[0]
        grad_near_w = jnp.concatenate([grad_w, to_first(grad_w)], axis=1)
        near_w = jnp.concatenate([act_w, to_first(act_w)], axis=1)
        back_hx = to_second(for_second(keep_hx, came_hx, shard))
        grad_far_w = to_second(grad_near_w)
        far_w = to_second(near_w)
        act_x, grad_x = middle(
            plane_total(keep_gx, after(came_gx, near_w, grad_near_w), back_gx, shard),
            plane_total(keep_hx, came_hx, back_hx, shard),
        )
        grad_near_x = jnp.concatenate([grad_x, to_first(grad_x)], axis=1)
        near_x = jnp.concatenate([act_x, to_first(act_x)], axis=1)
        grad_far_x = to_second(grad_near_x)
        far_x = to_second(near_x)

        def pair_sum(keep, go):
            return keep + along_gy(go, 1).astype(f32)

        def from_neighbour(sums):
            half = chips // 2 - 1
            sums = sums[: half * rows] + along_gy(sums[half * rows :].astype(bf16), 2).astype(f32)
            return [sums[i * rows : (i + 1) * rows] for i in range(half)]

        def from_far(held):
            held = [0.0] + held
            for step in reversed(bits(chips)[1:]):
                size = len(held) // 2
                came = [along_gy(h.astype(bf16), 2 * step).astype(f32) for h in held[size:]]
                held = [h + c for h, c in zip(held[:size], came)]
            return held[0]

        def at_home(sums):
            return sums[:rows] + along_gy(sums[rows:].astype(bf16), 2).astype(f32)

        keep, go, gain_w = normed_grad("normed_grad_w", grad_near_w, grad_far_w, w_up, normed_w, me)
        grad_sums_w = pair_sum(keep, go)
        keep, go = down_product("mlp_w", near_w, after(far_w, go), w_down, me)
        sums_w = pair_sum(keep, go)
        cot_w = after(cot_w, grad_sums_w, sums_w)
        down = weight_grad_down("wgrad_near", (near_w, near_x), (cot_w, cot_x), me, (0, 2), shard, units, None)
        keep, go, gain_x = normed_grad("normed_grad_x", grad_near_x, after(grad_far_x, down), w_up, normed_x, me)
        grad_sums_x = pair_sum(keep, go)
        keep, go = down_product("mlp_x", near_x, after(far_x, grad_sums_x), w_down, me)
        sums_x = pair_sum(keep, go)
        far_w = after(far_w, sums_x)
        grad_w_down = weight_grad_down("wgrad_far", (far_w, far_x), (cot_w, cot_x), me, (1, 3), shard, units, down)
        grad_held, held = from_neighbour(grad_sums_x), from_neighbour(sums_x)
        grad_w_up, grad_bias_up = weight_grad_up(
            (after(normed_w, grad_w_down, *grad_held, *held), normed_x),
            (grad_near_w, grad_near_x),
            (grad_far_w, grad_far_x),
            me,
            units,
        )
        grad_normed = at_home(grad_sums_w) + from_far(grad_held)
        mlp_out = (at_home(sums_w) + from_far(held) + bias_down).astype(bf16)
        grad_gain = (gain_w + gain_x)[0] / norm_gain
        for step in bits(n_gy):
            grad_gain = grad_gain + along_gy(grad_gain, step)

        grad_bias_down = jnp.sum(cot_w.astype(f32), axis=0) + jnp.sum(cot_x.astype(f32), axis=0)

        scaled = grad_normed * norm_gain
        sums = plane_sum(jnp.stack([jnp.sum(scaled, axis=1), jnp.sum(scaled * standard, axis=1)]))
        first_mean = (sums[0] / D)[:, None]
        second_mean = (sums[1] / D)[:, None]
        grad_patches = (inv_std * (scaled - first_mean - standard * second_mean)).astype(bf16)
        return mlp_out, grad_patches, grad_gain, grad_w_up, grad_bias_up[0], grad_w_down, grad_bias_down

    in_specs = (
        P("gy", "gx"),
        P("gx"),
        P("gx", "gy"),
        P("gy"),
        P("gy", "gx"),
        P("gx"),
        P("gy", "gx"),
    )
    out_specs = (
        P("gy", "gx"),
        P("gy", "gx"),
        P("gx"),
        P("gx", "gy"),
        P("gy"),
        P("gy", "gx"),
        P("gx"),
    )
    return jax.shard_map(shards, mesh=mesh, in_specs=in_specs, out_specs=out_specs, check_vma=False)
```

```python
import jax
import jax.numpy as jnp
from jax import lax
from jax.experimental import pallas as pl
from jax.experimental.pallas import tpu as pltpu
from jax.sharding import PartitionSpec as P

D = 6144

epsilon = 1e-06
inv_root_two = 0.7071067811865476
inv_root_two_pi = 0.3989422804014327

bf16 = jnp.bfloat16
f32 = jnp.float32
MIB = 1024 * 1024

NN = (((1,), (0,)), ((), ()))
NT = (((1,), (1,)), ((), ()))
TN = (((0,), (0,)), ((), ()))


def mm(left, right, dims):
    return lax.dot_general(left, right, dims, preferred_element_type=f32)


def call(kernel, name, out_shape, in_specs, out_specs, flops, moved, scratch=(), aliases=None, limit=8):
    return pl.pallas_call(
        kernel,
        name=name,
        out_shape=out_shape,
        in_specs=in_specs,
        out_specs=out_specs,
        scratch_shapes=scratch,
        input_output_aliases=aliases or {},
        compiler_params=pltpu.CompilerParams(vmem_limit_bytes=limit * MIB),
        cost_estimate=pl.CostEstimate(flops=0, bytes_accessed=0, transcendentals=0),
    )


IN_VMEM = pl.BlockSpec(memory_space=pltpu.VMEM)
IN_SMEM = pl.BlockSpec(memory_space=pltpu.SMEM)
IN_HBM = pl.BlockSpec(memory_space=pltpu.HBM)


def bits(n):
    return [1 << b for b in range(n.bit_length() - 1)]


def after(x, *others):
    return lax.optimization_barrier((x, *others))[0]


def block_at(me, rel, size):
    return pl.ds(pl.multiple_of((me ^ rel) * size, size), size)


def pieces_of(x_refs):
    return jnp.concatenate([x[...] for x in x_refs], axis=0)


def load_and_multiply(name, xs, w, me, shard, rels, dtype, by_rows):
    rows, depth = sum(x.shape[0] for x in xs), xs[0].shape[1]
    n, parts, whole = len(rels), 4, len(xs) > 1

    def kernel(me_ref, *refs):
        x_refs, (w_ref, o_ref, held_ref), sem = refs[: len(xs)], refs[len(xs) : len(xs) + 3], refs[-1]
        copies = {}
        for i, r in enumerate(rels):
            at, to = block_at(me_ref[0], r, shard), slice(i * shard, (i + 1) * shard)
            source, target = (w_ref.at[at, :], held_ref.at[to, :]) if by_rows else (w_ref.at[:, at], held_ref.at[:, to])
            size = source.shape[0] // parts
            for p in range(parts):
                span = pl.ds(p * size, size)
                copies[i, p] = pltpu.make_async_copy(source.at[span, :], target.at[span, :], sem.at[i, p])
                copies[i, p].start()
        x_ref = x_refs[0]
        if whole:
            x_ref = refs[len(xs) + 3]
            x_ref[...] = pieces_of(x_refs)
        for i in range(n):
            for p in range(parts):
                copies[i, p].wait()
            to = slice(i * shard, (i + 1) * shard)
            block = held_ref[to, :] if by_rows else held_ref[:, to]
            o_ref[:, to] = mm(x_ref[...], block, NT if by_rows else NN).astype(dtype)

    out_shape = [
        jax.ShapeDtypeStruct((rows, n * shard), dtype),
        pltpu.VMEM((n * shard, depth) if by_rows else (depth, n * shard), w.dtype),
    ]
    if whole:
        out_shape.append(jax.ShapeDtypeStruct((rows, depth), bf16))
    return call(
        kernel,
        name,
        out_shape,
        [IN_SMEM] + [IN_VMEM] * len(xs) + [IN_HBM],
        [IN_VMEM] * len(out_shape),
        2 * rows * depth * shard * n,
        2 * depth * shard * n,
        scratch=[pltpu.SemaphoreType.DMA((n, parts))],
    )(me, *xs, pltpu.with_memory_space_constraint(w, pltpu.HBM))


def multiply(name, xs, w_go, w_keep, shard, by_rows):
    rows, depth = sum(x.shape[0] for x in xs), xs[0].shape[1]

    def kernel(*refs):
        x_refs, (go_w, keep_w, go_ref, keep_ref, all_ref) = refs[: len(xs)], refs[len(xs) :]
        all_ref[...] = pieces_of(x_refs)
        for w_ref, o_ref in ((go_w, go_ref), (keep_w, keep_ref)):
            for c in (slice(0, shard), slice(shard, 2 * shard)):
                block = w_ref[c, :] if by_rows else w_ref[:, c]
                o_ref[:, c] = mm(all_ref[...], block, NT if by_rows else NN).astype(o_ref.dtype)

    return call(
        kernel,
        name,
        (
            jax.ShapeDtypeStruct((rows, 2 * shard), bf16),
            jax.ShapeDtypeStruct((rows, 2 * shard), f32),
            jax.ShapeDtypeStruct((rows, depth), bf16),
        ),
        [IN_VMEM] * (len(xs) + 2),
        [IN_VMEM] * 3,
        8 * rows * depth * shard,
        12 * rows * shard,
    )(*xs, w_go, w_keep)


def summed(near, far, w_ref, me, shard, cols, by_rows):
    total = None
    for r, ref, start in ((0, near, 0), (2, near, shard), (1, far, 0), (3, far, shard)):
        at = block_at(me, r, shard)
        block = w_ref[at, cols] if by_rows else w_ref[cols, at]
        term = mm(ref[:, start : start + shard], block, NN if by_rows else NT)
        total = term if total is None else total + term
    return total


def down_product(name, near, far, w_down, me):
    rows, wide = near.shape
    out = w_down.shape[1]
    half, shard, nb = rows // 2, wide // 2, 256

    def kernel(me_ref, near_ref, far_ref, w_ref, keep_ref, go_ref):
        for c in range(0, out, nb):
            cols = slice(c, c + nb)
            total = summed(near_ref, far_ref, w_ref, me_ref[0], shard, cols, True)
            keep_ref[:, cols] = total[:half]
            go_ref[:, cols] = total[half:].astype(bf16)

    return call(
        kernel,
        name,
        (jax.ShapeDtypeStruct((half, out), f32), jax.ShapeDtypeStruct((half, out), bf16)),
        [IN_SMEM] + [IN_VMEM] * 3,
        [IN_VMEM] * 2,
        4 * rows * wide * out,
        4 * rows * wide + 3 * rows * out,
    )(me, near, far, w_down)


def normed_grad(name, near, far, w_up, normed, me, gain=None):
    rows, wide = near.shape
    out = w_up.shape[0]
    half, shard, nb = rows // 2, wide // 2, 256
    more = () if gain is None else (gain,)

    def kernel(me_ref, near_ref, far_ref, w_ref, n_ref, *refs):
        keep_ref, go_ref, gain_ref = refs[-3:]
        for c in range(0, out, nb):
            cols = slice(c, c + nb)
            total = summed(near_ref, far_ref, w_ref, me_ref[0], shard, cols, False)
            keep_ref[:, cols] = total[:half]
            go_ref[:half, cols] = total[half:].astype(bf16)
            sums = jnp.sum(total * n_ref[:, cols].astype(f32), axis=0, keepdims=True)
            if more:
                sums += refs[0][:, cols]
                rounded = sums.astype(bf16).astype(f32)
                rest = (sums - rounded).astype(bf16).astype(f32)
                tail = [jnp.broadcast_to(rounded, (8, nb)), jnp.broadcast_to(rest, (8, nb))]
                go_ref[half:, cols] = jnp.concatenate(tail, axis=0).astype(bf16)
                sums = rounded + rest
            gain_ref[:, cols] = sums

    return call(
        kernel,
        name,
        (
            jax.ShapeDtypeStruct((half, out), f32),
            jax.ShapeDtypeStruct((half + 16 * len(more), out), bf16),
            jax.ShapeDtypeStruct((1, out), f32),
        ),
        [IN_SMEM] + [IN_VMEM] * (4 + len(more)),
        [IN_VMEM] * 3,
        4 * rows * wide * out,
        4 * rows * wide + 3 * rows * out,
    )(me, near, far, w_up, normed, *more)


def stream_out(steps, compute, place, buf, sem):
    copies = []
    for i in range(steps):
        if i >= 2:
            copies[i - 2].wait()
        buf[i % 2] = compute(i)
        copies.append(pltpu.make_async_copy(buf.at[i % 2], place(i), sem.at[i % 2]))
        copies[i].start()
    for c in copies[-2:]:
        c.wait()


def weight_grad_down(name, pieces, cots, me, rels, shard, units, so_far):
    nb = shard // 2
    out = cots[0].shape[1]
    tokens = sum(c.shape[0] for c in cots)
    steps = 2 * len(rels)

    def kernel(me_ref, p0, p1, c0, c1, *refs):
        o_ref, buf, sem = refs[-3:]

        def compute(i):
            cols = slice(i * nb, (i + 1) * nb)
            return mm(p0[:, cols], c0[...], TN) + mm(p1[:, cols], c1[...], TN)

        def place(i):
            start = (me_ref[0] ^ rels[i // 2]) * shard + (i % 2) * nb
            return o_ref.at[pl.ds(pl.multiple_of(start, nb), nb), :]

        stream_out(steps, compute, place, buf, sem)

    rest = () if so_far is None else (so_far,)
    return call(
        kernel,
        name,
        jax.ShapeDtypeStruct((units, out), f32),
        [IN_SMEM] + [IN_VMEM] * 4 + [IN_HBM] * len(rest),
        IN_HBM,
        2 * tokens * nb * steps * out,
        4 * nb * steps * out,
        scratch=[pltpu.VMEM((2, nb, out), f32), pltpu.SemaphoreType.DMA((2,))],
        aliases={5: 0} if rest else None,
        limit=12,
    )(me, *pieces, *cots, *rest)


def weight_grad_up(name, normed, nears, fars, me, units, span, so_far):
    out = normed[0].shape[1]
    tokens = sum(n.shape[0] for n in nears)
    shard = nears[0].shape[1] // 2
    nb = 256
    sums = so_far is None

    def kernel(me_ref, n0, n1, near0, near1, far0, far1, *refs):
        buf, sem = refs[-2:]
        o_ref = refs[0] if sums else refs[1]
        four = ((0, near0, near1, 0), (2, near0, near1, shard), (1, far0, far1, 0), (3, far0, far1, shard))
        copies = []
        for i, first in enumerate(span):
            if i >= 2:
                copies[i - 2].wait()
            rows = slice(first, first + nb)
            t0, t1 = n0[:, rows].T, n1[:, rows].T
            for r, p0, p1, start in four:
                at = slice(start, start + shard)
                term = mm(t0, p0[:, at], NN) + mm(t1, p1[:, at], NN)
                buf[i % 2, :, block_at(me_ref[0], r, shard)] = term
            copies.append(pltpu.make_async_copy(buf.at[i % 2], o_ref.at[rows, :], sem.at[i % 2]))
            copies[i].start()
        if sums:
            for r, p0, p1, start in four:
                at = slice(start, start + shard)
                total = jnp.sum(p0[:, at].astype(f32), axis=0, keepdims=True)
                total += jnp.sum(p1[:, at].astype(f32), axis=0, keepdims=True)
                refs[1][:, block_at(me_ref[0], r, shard)] = total
        for c in copies[-2:]:
            c.wait()

    out_shape = [jax.ShapeDtypeStruct((out, units), f32)]
    if sums:
        out_shape.append(jax.ShapeDtypeStruct((1, units), f32))
    return call(
        kernel,
        name,
        out_shape,
        [IN_SMEM] + [IN_VMEM] * 6 + ([] if sums else [IN_HBM]),
        [IN_HBM, IN_VMEM] if sums else [IN_HBM],
        2 * tokens * units * nb * len(span),
        4 * units * nb * len(span),
        scratch=[pltpu.VMEM((2, nb, units), f32), pltpu.SemaphoreType.DMA((2,))],
        aliases=None if sums else {7: 0},
        limit=14,
    )(me, *normed, *nears, *fars, *([] if sums else [so_far]))


def solution(mesh):
    n_gx, n_gy = mesh.shape["gx"], mesh.shape["gy"]
    both = ("gx", "gy")
    chips = n_gy // 2

    def across(first):
        pairs = []
        for gx in range(n_gx):
            for gy in range(n_gy):
                flip = 1 if (gy % 2 == 0) == first else 2
                pairs.append((gx * n_gy + gy, (gx ^ flip) * n_gy + gy))
        return pairs

    first_pairs, second_pairs = across(True), across(False)

    def to_first(x):
        return lax.ppermute(x, both, first_pairs)

    def to_second(x):
        return lax.ppermute(x, both, second_pairs)

    def along_gy(x, m):
        return lax.ppermute(x, "gy", [(i, i ^ m) for i in range(n_gy)])

    def along_gx(x, m):
        return lax.ppermute(x, "gx", [(i, i ^ m) for i in range(n_gx)])

    def plane_sum(x, least=1):
        for step in bits(n_gx)[least - 1 :]:
            x = x + along_gx(x, step)
        return x

    def over_groups(total):
        for step in bits(n_gx)[2:]:
            total = total + along_gx(total, step)
        return total

    def for_second(keep, came, shard):
        return (keep[:, shard:] + came[:, shard:].astype(f32)).astype(bf16)

    def plane_total(keep, came, back, shard):
        return over_groups(keep[:, :shard] + came[:, :shard].astype(f32) + back.astype(f32))

    def shards(patches, norm_gain, w_up, bias_up, w_down, bias_down, cotangent):
        rows = patches.shape[0]
        units = w_up.shape[1]
        shard = units // 4
        gx, gy = lax.axis_index("gx") % 4, lax.axis_index("gy")
        me = jnp.where(gy % 2 == 0, 2 * (gx % 2) + gx // 2, gx).astype(jnp.int32)
        bias = lax.dynamic_slice_in_dim(bias_up, me * shard, shard)
        me = me.reshape(1)

        w_up = pltpu.with_memory_space_constraint(w_up, pltpu.HBM)
        w_down = pltpu.with_memory_space_constraint(w_down, pltpu.HBM)

        def gather(own, first=()):
            z1 = along_gy(own, 2)
            if first:
                z1 = after(z1, *first)
            return [own, z1, along_gy(own, 1), along_gy(z1, 1)]

        def gather_far(own, first=()):
            even = [own]
            for step in bits(chips)[1:]:
                even += [along_gy(e, 2 * step) for e in even]
            even = even[1:]
            if first:
                even[0] = after(even[0], *first)
            even += [along_gy(e, 2) for e in even]
            even = jnp.concatenate(even)
            return [even, along_gy(even, 1)]

        cot_w = gather(cotangent)
        values = patches.astype(f32)
        totals = jnp.stack([jnp.sum(values, axis=1), jnp.sum(values * values, axis=1)])
        totals = totals + along_gx(totals, 1)
        late_down = pltpu.with_memory_space_constraint(w_down, pltpu.VMEM)
        late_up = pltpu.with_memory_space_constraint(w_up, pltpu.VMEM)
        go, down_go, cot_w = load_and_multiply("grad_act_w_go", cot_w, w_down, me, shard, (2, 3), bf16, True)
        came_gw = to_first(go)
        cot_x = gather_far(cotangent, [go])
        keep_gw, down_keep = load_and_multiply("grad_act_w_keep", [cot_w], w_down, me, shard, (0, 1), f32, True)
        totals = plane_sum(after(totals, go), 2)

        row_mean = (totals[0] / D)[:, None]
        variance = (totals[1] / D)[:, None] - row_mean * row_mean
        inv_std = lax.rsqrt(variance + epsilon)
        standard = (values - row_mean) * inv_std
        own = (standard * norm_gain).astype(bf16)
        second_gw = for_second(keep_gw, came_gw, shard)
        back_gw = to_second(second_gw)
        normed_w = gather(own, [second_gw])
        normed_x = gather_far(own)
        go, keep_gx, cot_x = multiply("grad_act_x", cot_x, down_go, down_keep, shard, True)
        came_gx = to_first(go)
        normed_w[0] = after(normed_w[0], go)
        go, up_go, normed_w = load_and_multiply("hidden_w_go", normed_w, w_up, me, shard, (2, 3), bf16, False)
        came_hw = to_first(go)
        keep_hw, up_keep = load_and_multiply("hidden_w_keep", [normed_w], w_up, me, shard, (0, 1), f32, False)
        second_gx = for_second(keep_gx, came_gx, shard)
        back_gx = to_second(second_gx)

        def middle(grad_act, hidden):
            hidden = hidden + bias
            upper = 0.5 * (1.0 + lax.erf(hidden * inv_root_two))
            act = (hidden * upper).astype(bf16)
            slope = upper + hidden * jnp.exp(-0.5 * hidden * hidden) * inv_root_two_pi
            return act, (grad_act * slope).astype(bf16)

        go, keep_hx, normed_x = multiply("hidden_x", normed_x, up_go, up_keep, shard, False)
        came_hx = to_first(go)
        second_hw = for_second(keep_hw, after(came_hw, second_gx, go), shard)
        back_hw = to_second(second_hw)
        second_hx = for_second(keep_hx, came_hx, shard)
        back_hx = to_second(second_hx)
        act_w, grad_w = middle(
            plane_total(keep_gw, after(came_gw, back_gx), back_gw, shard),
            plane_total(keep_hw, came_hw, after(back_hw, second_hx), shard),
        )
        grad_near_w = jnp.concatenate([grad_w, to_first(grad_w)], axis=1)
        near_w = jnp.concatenate([act_w, to_first(act_w)], axis=1)
        act_x, grad_x = middle(
            plane_total(keep_gx, after(came_gx, act_w, grad_w), back_gx, shard),
            plane_total(keep_hx, came_hx, back_hx, shard),
        )
        grad_near_x = jnp.concatenate([grad_x, after(to_first(grad_x), grad_near_w, near_w)], axis=1)
        near_x = jnp.concatenate([act_x, after(to_first(act_x), grad_near_x)], axis=1)
        grad_far_x = to_second(grad_near_x)
        far_x = to_second(near_x)
        grad_far_w = to_second(after(grad_near_w, near_x))
        far_w = to_second(after(near_w, near_x))

        def pair_sum(keep, go):
            return keep + along_gy(go, 1).astype(f32)

        def swap(block, m, gain):
            if gain is None:
                return along_gy(block.astype(bf16), m).astype(f32), None
            n = block.shape[0]
            rounded = lax.reduce_precision(gain, 8, 7)
            rest = lax.reduce_precision(gain - rounded, 8, 7)
            tail = [jnp.broadcast_to(g, (8, g.shape[1])) for g in (rounded, rest)]
            came = along_gy(jnp.concatenate([block] + tail).astype(bf16), m).astype(f32)
            return came[:n], (rounded + rest) + (came[n : n + 1] + came[n + 8 : n + 9])

        def from_neighbour(sums, gain=None, *first):
            half = chips // 2 - 1
            came, gain = swap(sums[half * rows :], 2, gain)
            came = after(came, *first) if first else came
            sums = sums[: half * rows] + came
            return [sums[i * rows : (i + 1) * rows] for i in range(half)], gain

        def from_far(held, gain=None):
            held = [0.0] + held
            for step in reversed(bits(chips)[1:]):
                size = len(held) // 2
                for i in range(size):
                    came, total = swap(held[size + i], 2 * step, gain if i == 0 else None)
                    held[i] = held[i] + came
                    if i == 0:
                        first = total
                held, gain = held[:size], first
            return held[0], gain

        down = weight_grad_down("wgrad_near", (near_w, near_x), (cot_w, cot_x), me, (0, 2), shard, units, None)
        keep, go, gain_x = normed_grad("normed_grad_x", grad_near_x, after(grad_far_x, down), late_up, normed_x, me)
        grad_sums_x = pair_sum(keep, go)
        keep, go = down_product("mlp_x", near_x, after(far_x, go), late_down, me)
        sums_x = pair_sum(keep, go)
        keep, go, gain = normed_grad(
            "normed_grad_w", grad_near_w, after(grad_far_w, go), late_up, normed_w, me, gain_x
        )
        n = keep.shape[0]
        normed = (after(normed_w, go, sums_x, grad_sums_x), normed_x)
        came = along_gy(go, 1).astype(f32)
        grad_sums_w = keep + came[:n]
        gain = gain + (came[n : n + 1] + came[n + 8 : n + 9])
        nears, fars = (grad_near_w, grad_near_x), (grad_far_w, grad_far_x)
        steps = range(0, patches.shape[1], 256)
        some, others = steps[: len(steps) // 2], steps[len(steps) // 2 :]
        grad_w_up, grad_bias_up = weight_grad_up("wgrad_up_1", normed, nears, fars, me, units, some, None)
        grad_held, _ = from_neighbour(grad_sums_x, None, grad_bias_up)
        held, _ = from_neighbour(sums_x, None, grad_bias_up)
        keep, go = down_product("mlp_w", near_w, after(far_w, grad_bias_up, grad_sums_w, *grad_held, *held), late_down, me)
        sums_w = pair_sum(keep, go)
        far_w = after(far_w, go, *held)
        grad_w_down = weight_grad_down("wgrad_far", (far_w, far_x), (cot_w, cot_x), me, (1, 3), shard, units, down)
        grad_far, _ = from_far(grad_held)
        came, gain = swap(grad_sums_w[rows:], 2, gain)
        grad_normed = grad_sums_w[:rows] + after(came, grad_w_down) + grad_far
        scaled = grad_normed * norm_gain
        sums = jnp.stack([jnp.sum(scaled, axis=1), jnp.sum(scaled * standard, axis=1)])
        normed = (after(normed_w, grad_w_down, sums_w, sums), normed_x)
        grad_w_up = weight_grad_up("wgrad_up_2", normed, nears, fars, me, units, others, grad_w_up)[0]
        sums = sums + after(along_gx(sums, 1), grad_w_up)
        mlp_home = sums_w[:rows] + after(along_gy(sums_w[rows:].astype(bf16), 2), grad_w_up).astype(f32)
        held = [after(h, grad_w_down) for h in held]
        mlp_out = (mlp_home + from_far(held)[0] + bias_down).astype(bf16)
        for step in bits(chips)[1:]:
            gain = gain + along_gy(gain, 2 * step)
        grad_gain = gain[0] / norm_gain

        grad_bias_down = jnp.sum(cot_w.astype(f32), axis=0) + jnp.sum(cot_x.astype(f32), axis=0)

        sums = plane_sum(sums, 2)
        first_mean = (sums[0] / D)[:, None]
        second_mean = (sums[1] / D)[:, None]
        grad_patches = (inv_std * (scaled - first_mean - standard * second_mean)).astype(bf16)
        return mlp_out, grad_patches, grad_gain, grad_w_up, grad_bias_up[0], grad_w_down, grad_bias_down

    in_specs = (
        P("gy", "gx"),
        P("gx"),
        P("gx", "gy"),
        P("gy"),
        P("gy", "gx"),
        P("gx"),
        P("gy", "gx"),
    )
    out_specs = (
        P("gy", "gx"),
        P("gy", "gx"),
        P("gx"),
        P("gx", "gy"),
        P("gy"),
        P("gy", "gx"),
        P("gx"),
    )
    return jax.shard_map(shards, mesh=mesh, in_specs=in_specs, out_specs=out_specs, check_vma=False)
```

```python
import jax
import jax.numpy as jnp
from jax import lax
from jax.experimental import pallas as pl
from jax.experimental.pallas import tpu as pltpu
from jax.sharding import PartitionSpec as P

D = 6144

epsilon = 1e-06
inv_root_two = 0.7071067811865476
inv_root_two_pi = 0.3989422804014327

bf16 = jnp.bfloat16
f32 = jnp.float32
MIB = 1024 * 1024

NN = (((1,), (0,)), ((), ()))
NT = (((1,), (1,)), ((), ()))
TN = (((0,), (0,)), ((), ()))


def mm(left, right, dims):
    return lax.dot_general(left, right, dims, preferred_element_type=f32)


def call(kernel, name, out_shape, in_specs, out_specs, flops, moved, scratch=(), aliases=None, limit=8):
    return pl.pallas_call(
        kernel,
        name=name,
        out_shape=out_shape,
        in_specs=in_specs,
        out_specs=out_specs,
        scratch_shapes=scratch,
        input_output_aliases=aliases or {},
        compiler_params=pltpu.CompilerParams(vmem_limit_bytes=limit * MIB),
        cost_estimate=pl.CostEstimate(flops=0, bytes_accessed=0, transcendentals=0),
    )


IN_VMEM = pl.BlockSpec(memory_space=pltpu.VMEM)
IN_SMEM = pl.BlockSpec(memory_space=pltpu.SMEM)
IN_HBM = pl.BlockSpec(memory_space=pltpu.HBM)


def bits(n):
    return [1 << b for b in range(n.bit_length() - 1)]


def after(x, *others):
    return lax.optimization_barrier((x, *others))[0]


def block_at(me, rel, size):
    return pl.ds(pl.multiple_of((me ^ rel) * size, size), size)


def pieces_of(x_refs):
    return jnp.concatenate([x[...] for x in x_refs], axis=0)


def load_and_multiply(name, xs, w, me, shard, rels, dtype, joined):
    rows, depth = sum(x.shape[0] for x in xs), xs[0].shape[1]
    n, parts = len(rels), 4

    def kernel(me_ref, *refs):
        x_refs, w_ref, out_refs, sem = refs[: len(xs)], refs[len(xs)], refs[len(xs) + 1 : -1], refs[-1]
        held_ref = out_refs[len(out_refs) - 2 if joined else -1]
        copies = {}
        for i, r in enumerate(rels):
            source, target = w_ref.at[block_at(me_ref[0], r, shard), :], held_ref.at[pl.ds(i * shard, shard), :]
            size = shard // parts
            for p in range(parts):
                span = pl.ds(p * size, size)
                copies[i, p] = pltpu.make_async_copy(source.at[span, :], target.at[span, :], sem.at[i, p])
                copies[i, p].start()
        if joined:
            out_refs[2][...] = pieces_of(x_refs)
            x_refs = out_refs[2:3]
        for i in range(n):
            for p in range(parts):
                copies[i, p].wait()
            to = slice(i * shard, (i + 1) * shard)
            for x_ref, o_ref in zip(x_refs, out_refs):
                o_ref[:, to] = mm(x_ref[...], held_ref[to, :], NT).astype(dtype)

    held = pltpu.VMEM((n * shard, depth), w.dtype)
    if joined:
        out_shape = [jax.ShapeDtypeStruct((rows, n * shard), dtype), held, jax.ShapeDtypeStruct((rows, depth), bf16)]
        scratch = []
    else:
        out_shape = [jax.ShapeDtypeStruct((x.shape[0], n * shard), dtype) for x in xs]
        scratch = [held]
    return call(
        kernel,
        name,
        out_shape,
        [IN_SMEM] + [IN_VMEM] * len(xs) + [IN_HBM],
        [IN_VMEM] * len(out_shape),
        2 * rows * depth * shard * n,
        2 * depth * shard * n,
        scratch=scratch + [pltpu.SemaphoreType.DMA((n, parts))],
        limit=8 if joined else 14,
    )(me, *xs, pltpu.with_memory_space_constraint(w, pltpu.HBM))


def multiply(name, xs, w, shard, by_rows, me=None):
    rows, depth = sum(x.shape[0] for x in xs), xs[0].shape[1]
    whole = me is not None
    more = (me,) if whole else ()

    def kernel(*refs):
        x_refs, w_ref, out_refs = refs[: len(xs)], refs[len(xs) + len(more)], refs[len(xs) + len(more) + 1 :]
        all_ref = out_refs[-1]
        all_ref[...] = pieces_of(x_refs)
        for i in range(4 if whole else 2):
            c = slice((i % 2) * shard, (i % 2 + 1) * shard)
            at = block_at(refs[len(xs)][0], (2, 3, 0, 1)[i], shard) if whole else c
            block = w_ref[at, :] if by_rows else w_ref[:, at]
            o_ref = out_refs[i // 2]
            o_ref[:, c] = mm(all_ref[...], block, NT if by_rows else NN).astype(o_ref.dtype)

    out_shape = [jax.ShapeDtypeStruct((rows, 2 * shard), bf16)]
    if whole:
        out_shape.append(jax.ShapeDtypeStruct((rows, 2 * shard), f32))
    out_shape.append(jax.ShapeDtypeStruct((rows, depth), bf16))
    return call(
        kernel,
        name,
        out_shape,
        [IN_VMEM] * len(xs) + [IN_SMEM] * len(more) + [IN_VMEM],
        [IN_VMEM] * len(out_shape),
        8 * rows * depth * shard,
        12 * rows * shard,
    )(*xs, *more, w)


def summed(near, far, w_ref, me, shard, cols, by_rows):
    total = None
    for r, ref, start in ((0, near, 0), (2, near, shard), (1, far, 0), (3, far, shard)):
        at = block_at(me, r, shard)
        block = w_ref[at, cols] if by_rows else w_ref[cols, at]
        term = mm(ref[:, start : start + shard], block, NN if by_rows else NT)
        total = term if total is None else total + term
    return total


def down_product(name, near, far, w_down, me):
    rows, wide = near.shape
    out = w_down.shape[1]
    half, shard, nb = rows // 2, wide // 2, 256

    def kernel(me_ref, near_ref, far_ref, w_ref, keep_ref, go_ref):
        for c in range(0, out, nb):
            cols = slice(c, c + nb)
            total = summed(near_ref, far_ref, w_ref, me_ref[0], shard, cols, True)
            keep_ref[:, cols] = total[:half]
            go_ref[:, cols] = total[half:].astype(bf16)

    return call(
        kernel,
        name,
        (jax.ShapeDtypeStruct((half, out), f32), jax.ShapeDtypeStruct((half, out), bf16)),
        [IN_SMEM] + [IN_VMEM] * 3,
        [IN_VMEM] * 2,
        4 * rows * wide * out,
        4 * rows * wide + 3 * rows * out,
    )(me, near, far, w_down)


def normed_grad(name, near, far, w_up, normed, me, gain=None):
    rows, wide = near.shape
    out = w_up.shape[0]
    half, shard, nb = rows // 2, wide // 2, 256
    more = () if gain is None else (gain,)

    def kernel(me_ref, near_ref, far_ref, w_ref, n_ref, *refs):
        keep_ref, go_ref, gain_ref = refs[-3:]
        for c in range(0, out, nb):
            cols = slice(c, c + nb)
            total = summed(near_ref, far_ref, w_ref, me_ref[0], shard, cols, False)
            keep_ref[:, cols] = total[:half]
            go_ref[:half, cols] = total[half:].astype(bf16)
            sums = jnp.sum(total * n_ref[:, cols].astype(f32), axis=0, keepdims=True)
            if more:
                sums += refs[0][:, cols]
                rounded = sums.astype(bf16).astype(f32)
                rest = (sums - rounded).astype(bf16).astype(f32)
                tail = [jnp.broadcast_to(rounded, (8, nb)), jnp.broadcast_to(rest, (8, nb))]
                go_ref[half:, cols] = jnp.concatenate(tail, axis=0).astype(bf16)
                sums = rounded + rest
            gain_ref[:, cols] = sums

    return call(
        kernel,
        name,
        (
            jax.ShapeDtypeStruct((half, out), f32),
            jax.ShapeDtypeStruct((half + 16 * len(more), out), bf16),
            jax.ShapeDtypeStruct((1, out), f32),
        ),
        [IN_SMEM] + [IN_VMEM] * (4 + len(more)),
        [IN_VMEM] * 3,
        4 * rows * wide * out,
        4 * rows * wide + 3 * rows * out,
    )(me, near, far, w_up, normed, *more)


def stream_out(steps, compute, place, buf, sem):
    copies = []
    for i in range(steps):
        if i >= 2:
            copies[i - 2].wait()
        buf[i % 2] = compute(i)
        copies.append(pltpu.make_async_copy(buf.at[i % 2], place(i), sem.at[i % 2]))
        copies[i].start()
    for c in copies[-2:]:
        c.wait()


def weight_grad_down(name, pieces, cots, me, rels, shard, units, so_far):
    nb = shard // 2
    out = cots[0].shape[1]
    tokens = sum(c.shape[0] for c in cots)
    steps = 2 * len(rels)

    def kernel(me_ref, p0, p1, c0, c1, *refs):
        o_ref, buf, sem = refs[-3:]

        def compute(i):
            cols = slice(i * nb, (i + 1) * nb)
            return mm(p0[:, cols], c0[...], TN) + mm(p1[:, cols], c1[...], TN)

        def place(i):
            start = (me_ref[0] ^ rels[i // 2]) * shard + (i % 2) * nb
            return o_ref.at[pl.ds(pl.multiple_of(start, nb), nb), :]

        stream_out(steps, compute, place, buf, sem)

    rest = () if so_far is None else (so_far,)
    return call(
        kernel,
        name,
        jax.ShapeDtypeStruct((units, out), f32),
        [IN_SMEM] + [IN_VMEM] * 4 + [IN_HBM] * len(rest),
        IN_HBM,
        2 * tokens * nb * steps * out,
        4 * nb * steps * out,
        scratch=[pltpu.VMEM((2, nb, out), f32), pltpu.SemaphoreType.DMA((2,))],
        aliases={5: 0} if rest else None,
        limit=12,
    )(me, *pieces, *cots, *rest)


def weight_grad_up(name, normed, nears, fars, me, units, span, so_far):
    out = normed[0].shape[1]
    tokens = sum(n.shape[0] for n in nears)
    shard = nears[0].shape[1] // 2
    nb = 256
    sums = so_far is None

    def kernel(me_ref, n0, n1, near0, near1, far0, far1, *refs):
        buf, sem = refs[-2:]
        o_ref = refs[0] if sums else refs[1]
        four = ((0, near0, near1, 0), (2, near0, near1, shard), (1, far0, far1, 0), (3, far0, far1, shard))
        copies = []
        for i, first in enumerate(span):
            if i >= 2:
                copies[i - 2].wait()
            rows = slice(first, first + nb)
            t0, t1 = n0[:, rows].T, n1[:, rows].T
            for r, p0, p1, start in four:
                at = slice(start, start + shard)
                term = mm(t0, p0[:, at], NN) + mm(t1, p1[:, at], NN)
                buf[i % 2, :, block_at(me_ref[0], r, shard)] = term
            copies.append(pltpu.make_async_copy(buf.at[i % 2], o_ref.at[rows, :], sem.at[i % 2]))
            copies[i].start()
        if sums:
            for r, p0, p1, start in four:
                at = slice(start, start + shard)
                total = jnp.sum(p0[:, at].astype(f32), axis=0, keepdims=True)
                total += jnp.sum(p1[:, at].astype(f32), axis=0, keepdims=True)
                refs[1][:, block_at(me_ref[0], r, shard)] = total
        for c in copies[-2:]:
            c.wait()

    out_shape = [jax.ShapeDtypeStruct((out, units), f32)]
    if sums:
        out_shape.append(jax.ShapeDtypeStruct((1, units), f32))
    return call(
        kernel,
        name,
        out_shape,
        [IN_SMEM] + [IN_VMEM] * 6 + ([] if sums else [IN_HBM]),
        [IN_HBM, IN_VMEM] if sums else [IN_HBM],
        2 * tokens * units * nb * len(span),
        4 * units * nb * len(span),
        scratch=[pltpu.VMEM((2, nb, units), f32), pltpu.SemaphoreType.DMA((2,))],
        aliases=None if sums else {7: 0},
        limit=14,
    )(me, *normed, *nears, *fars, *([] if sums else [so_far]))


def solution(mesh):
    n_gx, n_gy = mesh.shape["gx"], mesh.shape["gy"]
    both = ("gx", "gy")
    chips = n_gy // 2

    def across(first):
        pairs = []
        for gx in range(n_gx):
            for gy in range(n_gy):
                flip = 1 if (gy % 2 == 0) == first else 2
                pairs.append((gx * n_gy + gy, (gx ^ flip) * n_gy + gy))
        return pairs

    first_pairs, second_pairs = across(True), across(False)

    def to_first(x):
        return lax.ppermute(x, both, first_pairs)

    def to_second(x):
        return lax.ppermute(x, both, second_pairs)

    def along_gy(x, m):
        return lax.ppermute(x, "gy", [(i, i ^ m) for i in range(n_gy)])

    def along_gx(x, m):
        return lax.ppermute(x, "gx", [(i, i ^ m) for i in range(n_gx)])

    def plane_sum(x, least=1):
        for step in bits(n_gx)[least - 1 :]:
            x = x + along_gx(x, step)
        return x

    def over_groups(total):
        for step in bits(n_gx)[2:]:
            total = total + along_gx(total, step)
        return total

    def for_second(keep, came, shard):
        return (keep[:, shard:] + came[:, shard:].astype(f32)).astype(bf16)

    def plane_total(keep, came, back, shard):
        return over_groups(keep[:, :shard] + came[:, :shard].astype(f32) + back.astype(f32))

    def shards(patches, norm_gain, w_up, bias_up, w_down, bias_down, cotangent):
        rows = patches.shape[0]
        units = w_up.shape[1]
        shard = units // 4
        gx, gy = lax.axis_index("gx") % 4, lax.axis_index("gy")
        me = jnp.where(gy % 2 == 0, 2 * (gx % 2) + gx // 2, gx).astype(jnp.int32)
        bias = lax.dynamic_slice_in_dim(bias_up, me * shard, shard)
        me = me.reshape(1)

        w_up = pltpu.with_memory_space_constraint(w_up, pltpu.HBM)
        w_down = pltpu.with_memory_space_constraint(w_down, pltpu.HBM)

        def gather(own, first=()):
            z1 = along_gy(own, 2)
            if first:
                z1 = after(z1, *first)
            return [own, z1, along_gy(own, 1), along_gy(z1, 1)]

        def gather_far(own, first=()):
            even = [own]
            for step in bits(chips)[1:]:
                even += [along_gy(e, 2 * step) for e in even]
            even = even[1:]
            if first:
                even[0] = after(even[0], *first)
            return even + [along_gy(e, 2) for e in even]

        def swapped(even, first):
            even = even[:-1] + [after(even[-1], *first)]
            even = jnp.concatenate(even)
            return [even, along_gy(even, 1)]

        cot_w = gather(cotangent)
        values = patches.astype(f32)
        totals = jnp.stack([jnp.sum(values, axis=1), jnp.sum(values * values, axis=1)])
        totals = totals + along_gx(totals, 1)
        late_down = pltpu.with_memory_space_constraint(w_down, pltpu.VMEM)
        late_up = pltpu.with_memory_space_constraint(w_up, pltpu.VMEM)
        go, down_go, cot_w = load_and_multiply("grad_act_w_go", cot_w, w_down, me, shard, (2, 3), bf16, True)
        came_gw = to_first(go)
        cot_x = swapped(gather_far(cotangent, [go]), [go])
        totals = plane_sum(after(totals, go), 2)

        row_mean = (totals[0] / D)[:, None]
        variance = (totals[1] / D)[:, None] - row_mean * row_mean
        inv_std = lax.rsqrt(variance + epsilon)
        standard = (values - row_mean) * inv_std
        own = (standard * norm_gain).astype(bf16)
        go, cot_x = multiply("grad_act_x_go", cot_x, down_go, shard, True)
        came_gx = to_first(go)
        keep_gw, keep_gx = load_and_multiply("grad_act_keep", [cot_w, cot_x], w_down, me, shard, (0, 1), f32, False)
        second_gw = for_second(keep_gw, came_gw, shard)
        back_gw = to_second(second_gw)
        normed_w = gather(own, [go])
        normed_even = gather_far(own, [keep_gw])
        second_gx = for_second(keep_gx, came_gx, shard)
        back_gx = to_second(second_gx)
        normed_w[0] = after(normed_w[0], second_gw, second_gx)
        go, keep_hw, normed_w = multiply("hidden_w", normed_w, late_up, shard, False, me)
        came_hw = to_first(go)
        normed_x = swapped(normed_even, [go])

        def middle(grad_act, hidden):
            hidden = hidden + bias
            upper = 0.5 * (1.0 + lax.erf(hidden * inv_root_two))
            act = (hidden * upper).astype(bf16)
            slope = upper + hidden * jnp.exp(-0.5 * hidden * hidden) * inv_root_two_pi
            return act, (grad_act * slope).astype(bf16)

        normed_x[0] = after(normed_x[0], back_gw)
        go, keep_hx, normed_x = multiply("hidden_x", normed_x, late_up, shard, False, me)
        came_hx = to_first(go)
        second_hw = for_second(keep_hw, after(came_hw, back_gx, go), shard)
        back_hw = to_second(second_hw)
        second_hx = for_second(keep_hx, came_hx, shard)
        back_hx = to_second(second_hx)
        act_w, grad_w = middle(
            plane_total(keep_gw, came_gw, back_gw, shard),
            plane_total(keep_hw, came_hw, after(back_hw, second_hx), shard),
        )
        grad_near_w = jnp.concatenate([grad_w, to_first(grad_w)], axis=1)
        near_w = jnp.concatenate([act_w, to_first(act_w)], axis=1)
        act_x, grad_x = middle(
            plane_total(keep_gx, after(came_gx, act_w, grad_w), back_gx, shard),
            plane_total(keep_hx, came_hx, back_hx, shard),
        )
        grad_near_x = jnp.concatenate([grad_x, after(to_first(grad_x), grad_near_w, near_w)], axis=1)
        near_x = jnp.concatenate([act_x, after(to_first(act_x), grad_near_x)], axis=1)
        grad_far_x = to_second(grad_near_x)
        far_x = to_second(near_x)
        grad_far_w = to_second(after(grad_near_w, grad_near_x))
        far_w = to_second(after(near_w, near_x))

        def pair_sum(keep, go):
            return keep + along_gy(go, 1).astype(f32)

        def swap(block, m, gain):
            if gain is None:
                return along_gy(block.astype(bf16), m).astype(f32), None
            n = block.shape[0]
            rounded = lax.reduce_precision(gain, 8, 7)
            rest = lax.reduce_precision(gain - rounded, 8, 7)
            tail = [jnp.broadcast_to(g, (8, g.shape[1])) for g in (rounded, rest)]
            came = along_gy(jnp.concatenate([block] + tail).astype(bf16), m).astype(f32)
            return came[:n], (rounded + rest) + (came[n : n + 1] + came[n + 8 : n + 9])

        def from_neighbour(sums, gain=None, *first):
            half = chips // 2 - 1
            came, gain = swap(sums[half * rows :], 2, gain)
            came = after(came, *first) if first else came
            sums = sums[: half * rows] + came
            return [sums[i * rows : (i + 1) * rows] for i in range(half)], gain

        def from_far(held, gain=None):
            held = [0.0] + held
            for step in reversed(bits(chips)[1:]):
                size = len(held) // 2
                for i in range(size):
                    came, total = swap(held[size + i], 2 * step, gain if i == 0 else None)
                    held[i] = held[i] + came
                    if i == 0:
                        first = total
                held, gain = held[:size], first
            return held[0], gain

        down = weight_grad_down("wgrad_near", (near_w, near_x), (cot_w, cot_x), me, (0, 2), shard, units, None)
        keep, go, gain_x = normed_grad("normed_grad_x", grad_near_x, after(grad_far_x, down), late_up, normed_x, me)
        grad_sums_x = pair_sum(keep, go)
        keep, go, gain = normed_grad(
            "normed_grad_w", grad_near_w, after(grad_far_w, go), late_up, normed_w, me, gain_x
        )
        n = keep.shape[0]
        nears, fars = (grad_near_w, grad_near_x), (grad_far_w, grad_far_x)
        steps = range(0, patches.shape[1], 256)
        some, others = steps[: len(steps) // 2], steps[len(steps) // 2 :]
        normed = (after(normed_w, go), normed_x)
        grad_w_up, grad_bias_up = weight_grad_up("wgrad_up_1", normed, nears, fars, me, units, some, None)
        came = along_gy(go, 1).astype(f32)
        grad_sums_w = keep + came[:n]
        gain = gain + (came[n : n + 1] + came[n + 8 : n + 9])
        keep, go = down_product("mlp_x", near_x, after(far_x, grad_bias_up), late_down, me)
        sums_x = pair_sum(keep, go)
        grad_held, _ = from_neighbour(grad_sums_x)
        normed = (after(normed_w, go, grad_sums_w, sums_x, *grad_held), normed_x)
        grad_w_up = weight_grad_up("wgrad_up_2", normed, nears, fars, me, units, others, grad_w_up)[0]
        held, _ = from_neighbour(sums_x, None, grad_w_up)
        keep, go = down_product("mlp_w", near_w, after(far_w, grad_w_up), late_down, me)
        sums_w = pair_sum(keep, go)
        far_w = after(far_w, go, sums_w)
        grad_w_down = weight_grad_down("wgrad_far", (far_w, far_x), (cot_w, cot_x), me, (1, 3), shard, units, down)
        grad_far, _ = from_far(grad_held)
        came, gain = swap(grad_sums_w[rows:], 2, gain)
        grad_normed = grad_sums_w[:rows] + after(came, go) + grad_far
        scaled = grad_normed * norm_gain
        sums = jnp.stack([jnp.sum(scaled, axis=1), jnp.sum(scaled * standard, axis=1)])
        sums = sums + after(along_gx(sums, 1), grad_w_down)
        mlp_home = sums_w[:rows] + after(along_gy(sums_w[rows:].astype(bf16), 2), grad_w_down).astype(f32)
        held = [after(h, grad_w_up) for h in held]
        mlp_out = (mlp_home + from_far(held)[0] + bias_down).astype(bf16)
        for step in bits(chips)[1:]:
            gain = gain + along_gy(gain, 2 * step)
        grad_gain = gain[0] / norm_gain

        grad_bias_down = jnp.sum(cot_w.astype(f32), axis=0) + jnp.sum(cot_x.astype(f32), axis=0)

        sums = plane_sum(sums, 2)
        first_mean = (sums[0] / D)[:, None]
        second_mean = (sums[1] / D)[:, None]
        grad_patches = (inv_std * (scaled - first_mean - standard * second_mean)).astype(bf16)
        return mlp_out, grad_patches, grad_gain, grad_w_up, grad_bias_up[0], grad_w_down, grad_bias_down

    in_specs = (
        P("gy", "gx"),
        P("gx"),
        P("gx", "gy"),
        P("gy"),
        P("gy", "gx"),
        P("gx"),
        P("gy", "gx"),
    )
    out_specs = (
        P("gy", "gx"),
        P("gy", "gx"),
        P("gx"),
        P("gx", "gy"),
        P("gy"),
        P("gy", "gx"),
        P("gx"),
    )
    return jax.shard_map(shards, mesh=mesh, in_specs=in_specs, out_specs=out_specs, check_vma=False)
```

```python
import jax
import jax.numpy as jnp
from jax import lax
from jax.experimental import pallas as pl
from jax.experimental.pallas import tpu as pltpu
from jax.sharding import PartitionSpec as P

D = 6144

epsilon = 1e-06
inv_root_two = 0.7071067811865476
inv_root_two_pi = 0.3989422804014327

bf16 = jnp.bfloat16
f32 = jnp.float32
MIB = 1024 * 1024

NN = (((1,), (0,)), ((), ()))
NT = (((1,), (1,)), ((), ()))
TN = (((0,), (0,)), ((), ()))


def mm(left, right, dims):
    return lax.dot_general(left, right, dims, preferred_element_type=f32)


def call(kernel, name, out_shape, in_specs, out_specs, flops, moved, scratch=(), aliases=None, limit=8):
    return pl.pallas_call(
        kernel,
        name=name,
        out_shape=out_shape,
        in_specs=in_specs,
        out_specs=out_specs,
        scratch_shapes=scratch,
        input_output_aliases=aliases or {},
        compiler_params=pltpu.CompilerParams(vmem_limit_bytes=limit * MIB),
        cost_estimate=pl.CostEstimate(flops=0, bytes_accessed=0, transcendentals=0),
    )


IN_VMEM = pl.BlockSpec(memory_space=pltpu.VMEM)
IN_SMEM = pl.BlockSpec(memory_space=pltpu.SMEM)
IN_HBM = pl.BlockSpec(memory_space=pltpu.HBM)


def bits(n):
    return [1 << b for b in range(n.bit_length() - 1)]


def after(x, *others):
    return lax.optimization_barrier((x, *others))[0]


def block_at(me, rel, size):
    return pl.ds(pl.multiple_of((me ^ rel) * size, size), size)


def pieces_of(x_refs):
    return jnp.concatenate([x[...] for x in x_refs], axis=0)


def load_and_multiply(name, xs, w, me, shard, rels, dtype, joined):
    rows, depth = sum(x.shape[0] for x in xs), xs[0].shape[1]
    n, parts = len(rels), 4

    def kernel(me_ref, *refs):
        x_refs, w_ref, out_refs, sem = refs[: len(xs)], refs[len(xs)], refs[len(xs) + 1 : -1], refs[-1]
        held_ref = out_refs[len(out_refs) - 2 if joined else -1]
        copies = {}
        for i, r in enumerate(rels):
            source, target = w_ref.at[block_at(me_ref[0], r, shard), :], held_ref.at[pl.ds(i * shard, shard), :]
            size = shard // parts
            for p in range(parts):
                span = pl.ds(p * size, size)
                copies[i, p] = pltpu.make_async_copy(source.at[span, :], target.at[span, :], sem.at[i, p])
                copies[i, p].start()
        if joined:
            out_refs[2][...] = pieces_of(x_refs)
            x_refs = out_refs[2:3]
        for i in range(n):
            for p in range(parts):
                copies[i, p].wait()
            to = slice(i * shard, (i + 1) * shard)
            for x_ref, o_ref in zip(x_refs, out_refs):
                o_ref[:, to] = mm(x_ref[...], held_ref[to, :], NT).astype(dtype)

    held = pltpu.VMEM((n * shard, depth), w.dtype)
    if joined:
        out_shape = [jax.ShapeDtypeStruct((rows, n * shard), dtype), held, jax.ShapeDtypeStruct((rows, depth), bf16)]
        scratch = []
    else:
        out_shape = [jax.ShapeDtypeStruct((x.shape[0], n * shard), dtype) for x in xs]
        scratch = [held]
    return call(
        kernel,
        name,
        out_shape,
        [IN_SMEM] + [IN_VMEM] * len(xs) + [IN_HBM],
        [IN_VMEM] * len(out_shape),
        2 * rows * depth * shard * n,
        2 * depth * shard * n,
        scratch=scratch + [pltpu.SemaphoreType.DMA((n, parts))],
        limit=8 if joined else 14,
    )(me, *xs, pltpu.with_memory_space_constraint(w, pltpu.HBM))


def multiply(name, xs, w, shard, by_rows, me=None):
    rows, depth = sum(x.shape[0] for x in xs), xs[0].shape[1]
    whole = me is not None
    more = (me,) if whole else ()

    def kernel(*refs):
        x_refs, w_ref, out_refs = refs[: len(xs)], refs[len(xs) + len(more)], refs[len(xs) + len(more) + 1 :]
        all_ref = out_refs[-1]
        all_ref[...] = pieces_of(x_refs)
        for i in range(4 if whole else 2):
            c = slice((i % 2) * shard, (i % 2 + 1) * shard)
            at = block_at(refs[len(xs)][0], (2, 3, 0, 1)[i], shard) if whole else c
            block = w_ref[at, :] if by_rows else w_ref[:, at]
            o_ref = out_refs[i // 2]
            o_ref[:, c] = mm(all_ref[...], block, NT if by_rows else NN).astype(o_ref.dtype)

    out_shape = [jax.ShapeDtypeStruct((rows, 2 * shard), bf16)]
    if whole:
        out_shape.append(jax.ShapeDtypeStruct((rows, 2 * shard), f32))
    out_shape.append(jax.ShapeDtypeStruct((rows, depth), bf16))
    return call(
        kernel,
        name,
        out_shape,
        [IN_VMEM] * len(xs) + [IN_SMEM] * len(more) + [IN_VMEM],
        [IN_VMEM] * len(out_shape),
        8 * rows * depth * shard,
        12 * rows * shard,
    )(*xs, *more, w)


def summed(near, far, w_ref, me, shard, cols, by_rows):
    total = None
    for r, ref, start in ((0, near, 0), (2, near, shard), (1, far, 0), (3, far, shard)):
        at = block_at(me, r, shard)
        block = w_ref[at, cols] if by_rows else w_ref[cols, at]
        term = mm(ref[:, start : start + shard], block, NN if by_rows else NT)
        total = term if total is None else total + term
    return total


def down_product(name, near, far, w_down, me):
    rows, wide = near.shape
    out = w_down.shape[1]
    half, shard, nb = rows // 2, wide // 2, 256

    def kernel(me_ref, near_ref, far_ref, w_ref, keep_ref, go_ref):
        for c in range(0, out, nb):
            cols = slice(c, c + nb)
            total = summed(near_ref, far_ref, w_ref, me_ref[0], shard, cols, True)
            keep_ref[:, cols] = total[:half]
            go_ref[:, cols] = total[half:].astype(bf16)

    return call(
        kernel,
        name,
        (jax.ShapeDtypeStruct((half, out), f32), jax.ShapeDtypeStruct((half, out), bf16)),
        [IN_SMEM] + [IN_VMEM] * 3,
        [IN_VMEM] * 2,
        4 * rows * wide * out,
        4 * rows * wide + 3 * rows * out,
    )(me, near, far, w_down)


def normed_grad(name, near, far, w_up, normed, me, gain=None):
    rows, wide = near.shape
    out = w_up.shape[0]
    half, shard, nb = rows // 2, wide // 2, 256
    more = () if gain is None else (gain,)

    def kernel(me_ref, near_ref, far_ref, w_ref, n_ref, *refs):
        keep_ref, go_ref, gain_ref = refs[-3:]
        for c in range(0, out, nb):
            cols = slice(c, c + nb)
            total = summed(near_ref, far_ref, w_ref, me_ref[0], shard, cols, False)
            keep_ref[:, cols] = total[:half]
            go_ref[:half, cols] = total[half:].astype(bf16)
            sums = jnp.sum(total * n_ref[:, cols].astype(f32), axis=0, keepdims=True)
            if more:
                sums += refs[0][:, cols]
                rounded = sums.astype(bf16).astype(f32)
                rest = (sums - rounded).astype(bf16).astype(f32)
                tail = [jnp.broadcast_to(rounded, (8, nb)), jnp.broadcast_to(rest, (8, nb))]
                go_ref[half:, cols] = jnp.concatenate(tail, axis=0).astype(bf16)
                sums = rounded + rest
            gain_ref[:, cols] = sums

    return call(
        kernel,
        name,
        (
            jax.ShapeDtypeStruct((half, out), f32),
            jax.ShapeDtypeStruct((half + 16 * len(more), out), bf16),
            jax.ShapeDtypeStruct((1, out), f32),
        ),
        [IN_SMEM] + [IN_VMEM] * (4 + len(more)),
        [IN_VMEM] * 3,
        4 * rows * wide * out,
        4 * rows * wide + 3 * rows * out,
    )(me, near, far, w_up, normed, *more)


def stream_out(steps, compute, place, buf, sem):
    copies = []
    for i in range(steps):
        if i >= 2:
            copies[i - 2].wait()
        buf[i % 2] = compute(i)
        copies.append(pltpu.make_async_copy(buf.at[i % 2], place(i), sem.at[i % 2]))
        copies[i].start()
    for c in copies[-2:]:
        c.wait()


def weight_grad_down(name, pieces, cots, me, rels, shard, units, so_far):
    nb = shard // 2
    out = cots[0].shape[1]
    tokens = sum(c.shape[0] for c in cots)
    steps = 2 * len(rels)

    def kernel(me_ref, p0, p1, c0, c1, *refs):
        o_ref, buf, sem = refs[-3:]

        def compute(i):
            cols = slice(i * nb, (i + 1) * nb)
            return mm(p0[:, cols], c0[...], TN) + mm(p1[:, cols], c1[...], TN)

        def place(i):
            start = (me_ref[0] ^ rels[i // 2]) * shard + (i % 2) * nb
            return o_ref.at[pl.ds(pl.multiple_of(start, nb), nb), :]

        stream_out(steps, compute, place, buf, sem)

    rest = () if so_far is None else (so_far,)
    return call(
        kernel,
        name,
        jax.ShapeDtypeStruct((units, out), f32),
        [IN_SMEM] + [IN_VMEM] * 4 + [IN_HBM] * len(rest),
        IN_HBM,
        2 * tokens * nb * steps * out,
        4 * nb * steps * out,
        scratch=[pltpu.VMEM((2, nb, out), f32), pltpu.SemaphoreType.DMA((2,))],
        aliases={5: 0} if rest else None,
        limit=12,
    )(me, *pieces, *cots, *rest)


def weight_grad_up(name, normed, nears, fars, me, units, span, so_far):
    out = normed[0].shape[1]
    tokens = sum(n.shape[0] for n in nears)
    shard = nears[0].shape[1] // 2
    nb = 256
    sums = so_far is None

    def kernel(me_ref, n0, n1, near0, near1, far0, far1, *refs):
        buf, sem = refs[-2:]
        o_ref = refs[0] if sums else refs[1]
        four = ((0, near0, near1, 0), (2, near0, near1, shard), (1, far0, far1, 0), (3, far0, far1, shard))
        copies = []
        for i, first in enumerate(span):
            if i >= 2:
                copies[i - 2].wait()
            rows = slice(first, first + nb)
            t0, t1 = n0[:, rows].T, n1[:, rows].T
            for r, p0, p1, start in four:
                at = slice(start, start + shard)
                term = mm(t0, p0[:, at], NN) + mm(t1, p1[:, at], NN)
                buf[i % 2, :, block_at(me_ref[0], r, shard)] = term
            copies.append(pltpu.make_async_copy(buf.at[i % 2], o_ref.at[rows, :], sem.at[i % 2]))
            copies[i].start()
        if sums:
            for r, p0, p1, start in four:
                at = slice(start, start + shard)
                total = jnp.sum(p0[:, at].astype(f32), axis=0, keepdims=True)
                total += jnp.sum(p1[:, at].astype(f32), axis=0, keepdims=True)
                refs[1][:, block_at(me_ref[0], r, shard)] = total
        for c in copies[-2:]:
            c.wait()

    out_shape = [jax.ShapeDtypeStruct((out, units), f32)]
    if sums:
        out_shape.append(jax.ShapeDtypeStruct((1, units), f32))
    return call(
        kernel,
        name,
        out_shape,
        [IN_SMEM] + [IN_VMEM] * 6 + ([] if sums else [IN_HBM]),
        [IN_HBM, IN_VMEM] if sums else [IN_HBM],
        2 * tokens * units * nb * len(span),
        4 * units * nb * len(span),
        scratch=[pltpu.VMEM((2, nb, units), f32), pltpu.SemaphoreType.DMA((2,))],
        aliases=None if sums else {7: 0},
        limit=14,
    )(me, *normed, *nears, *fars, *([] if sums else [so_far]))


def solution(mesh):
    n_gx, n_gy = mesh.shape["gx"], mesh.shape["gy"]
    both = ("gx", "gy")
    chips = n_gy // 2

    def across(first):
        pairs = []
        for gx in range(n_gx):
            for gy in range(n_gy):
                flip = 1 if (gy % 2 == 0) == first else 2
                pairs.append((gx * n_gy + gy, (gx ^ flip) * n_gy + gy))
        return pairs

    first_pairs, second_pairs = across(True), across(False)

    def to_first(x):
        return lax.ppermute(x, both, first_pairs)

    def to_second(x):
        return lax.ppermute(x, both, second_pairs)

    def along_gy(x, m):
        return lax.ppermute(x, "gy", [(i, i ^ m) for i in range(n_gy)])

    def along_gx(x, m):
        return lax.ppermute(x, "gx", [(i, i ^ m) for i in range(n_gx)])

    def plane_sum(x, least=1):
        for step in bits(n_gx)[least - 1 :]:
            x = x + along_gx(x, step)
        return x

    def over_groups(total):
        for step in bits(n_gx)[2:]:
            total = total + along_gx(total, step)
        return total

    def for_second(keep, came, shard):
        return (keep[:, shard:] + came[:, shard:].astype(f32)).astype(bf16)

    def plane_total(keep, came, back, shard):
        return over_groups(keep[:, :shard] + came[:, :shard].astype(f32) + back.astype(f32))

    def shards(patches, norm_gain, w_up, bias_up, w_down, bias_down, cotangent):
        rows = patches.shape[0]
        units = w_up.shape[1]
        shard = units // 4
        gx, gy = lax.axis_index("gx") % 4, lax.axis_index("gy")
        me = jnp.where(gy % 2 == 0, 2 * (gx % 2) + gx // 2, gx).astype(jnp.int32)
        bias = lax.dynamic_slice_in_dim(bias_up, me * shard, shard)
        me = me.reshape(1)

        w_up = pltpu.with_memory_space_constraint(w_up, pltpu.HBM)
        w_down = pltpu.with_memory_space_constraint(w_down, pltpu.HBM)

        def gather(own, first=()):
            z1 = along_gy(own, 2)
            if first:
                z1 = after(z1, *first)
            return [own, z1, along_gy(own, 1), along_gy(z1, 1)]

        def gather_far(own, first=()):
            even = [own]
            for step in bits(chips)[1:]:
                even += [along_gy(e, 2 * step) for e in even]
            even = even[1:]
            if first:
                even[0] = after(even[0], *first)
            return even + [along_gy(e, 2) for e in even]

        def swapped(even, first):
            even = even[:-1] + [after(even[-1], *first)]
            even = jnp.concatenate(even)
            return [even, along_gy(even, 1)]

        cot_w = gather(cotangent)
        values = patches.astype(f32)
        totals = jnp.stack([jnp.sum(values, axis=1), jnp.sum(values * values, axis=1)])
        totals = totals + along_gx(totals, 1)
        late_down = pltpu.with_memory_space_constraint(w_down, pltpu.VMEM)
        late_up = pltpu.with_memory_space_constraint(w_up, pltpu.VMEM)
        go, down_go, cot_w = load_and_multiply("grad_act_w_go", cot_w, w_down, me, shard, (2, 3), bf16, True)
        came_gw = to_first(go)
        cot_x = swapped(gather_far(cotangent, [go]), [go])
        totals = plane_sum(after(totals, go), 2)

        row_mean = (totals[0] / D)[:, None]
        variance = (totals[1] / D)[:, None] - row_mean * row_mean
        inv_std = lax.rsqrt(variance + epsilon)
        standard = (values - row_mean) * inv_std
        own = (standard * norm_gain).astype(bf16)
        go, cot_x = multiply("grad_act_x_go", cot_x, down_go, shard, True)
        came_gx = to_first(go)
        keep_gw, keep_gx = load_and_multiply("grad_act_keep", [cot_w, cot_x], w_down, me, shard, (0, 1), f32, False)
        second_gw = for_second(keep_gw, came_gw, shard)
        back_gw = to_second(second_gw)
        normed_w = gather(own, [go])
        normed_even = gather_far(own, [keep_gw])
        second_gx = for_second(keep_gx, came_gx, shard)
        back_gx = to_second(second_gx)
        normed_w[0] = after(normed_w[0], second_gw, second_gx)
        go, keep_hw, normed_w = multiply("hidden_w", normed_w, late_up, shard, False, me)
        came_hw = to_first(go)
        normed_x = swapped(normed_even, [go])

        def middle(grad_act, hidden):
            hidden = hidden + bias
            upper = 0.5 * (1.0 + lax.erf(hidden * inv_root_two))
            act = (hidden * upper).astype(bf16)
            slope = upper + hidden * jnp.exp(-0.5 * hidden * hidden) * inv_root_two_pi
            return act, (grad_act * slope).astype(bf16)

        normed_x[0] = after(normed_x[0], back_gw)
        go, keep_hx, normed_x = multiply("hidden_x", normed_x, late_up, shard, False, me)
        came_hx = to_first(go)
        second_hw = for_second(keep_hw, after(came_hw, back_gx, go), shard)
        back_hw = to_second(second_hw)
        second_hx = for_second(keep_hx, came_hx, shard)
        back_hx = to_second(second_hx)
        act_w, grad_w = middle(
            plane_total(keep_gw, came_gw, back_gw, shard),
            plane_total(keep_hw, came_hw, after(back_hw, second_hx), shard),
        )
        grad_near_w = jnp.concatenate([grad_w, to_first(grad_w)], axis=1)
        near_w = jnp.concatenate([act_w, to_first(act_w)], axis=1)
        act_x, grad_x = middle(
            plane_total(keep_gx, after(came_gx, act_w, grad_w), back_gx, shard),
            plane_total(keep_hx, came_hx, back_hx, shard),
        )
        grad_near_x = jnp.concatenate([grad_x, after(to_first(grad_x), grad_near_w, near_w)], axis=1)
        near_x = jnp.concatenate([act_x, after(to_first(act_x), grad_near_x)], axis=1)
        grad_far_x = to_second(grad_near_x)
        far_x = to_second(near_x)
        grad_far_w = to_second(after(grad_near_w, grad_near_x))
        far_w = to_second(after(near_w, near_x))

        def pair_sum(keep, go):
            return keep + along_gy(go, 1).astype(f32)

        def swap(block, m, gain):
            if gain is None:
                return along_gy(block.astype(bf16), m).astype(f32), None
            n = block.shape[0]
            rounded = lax.reduce_precision(gain, 8, 7)
            rest = lax.reduce_precision(gain - rounded, 8, 7)
            tail = [jnp.broadcast_to(g, (8, g.shape[1])) for g in (rounded, rest)]
            came = along_gy(jnp.concatenate([block] + tail).astype(bf16), m).astype(f32)
            return came[:n], (rounded + rest) + (came[n : n + 1] + came[n + 8 : n + 9])

        def from_neighbour(sums, gain=None, *first):
            half = chips // 2 - 1
            came, gain = swap(sums[half * rows :], 2, gain)
            came = after(came, *first) if first else came
            sums = sums[: half * rows] + came
            return [sums[i * rows : (i + 1) * rows] for i in range(half)], gain

        def from_far(held, gain=None):
            held = [0.0] + held
            for step in reversed(bits(chips)[1:]):
                size = len(held) // 2
                for i in range(size):
                    came, total = swap(held[size + i], 2 * step, gain if i == 0 else None)
                    held[i] = held[i] + came
                    if i == 0:
                        first = total
                held, gain = held[:size], first
            return held[0], gain

        down = weight_grad_down("wgrad_near", (near_w, near_x), (cot_w, cot_x), me, (0, 2), shard, units, None)
        keep, go, gain_x = normed_grad("normed_grad_x", grad_near_x, after(grad_far_x, down), late_up, normed_x, me)
        grad_sums_x = pair_sum(keep, go)
        keep, go, gain = normed_grad(
            "normed_grad_w", grad_near_w, after(grad_far_w, go), late_up, normed_w, me, gain_x
        )
        n = keep.shape[0]
        nears, fars = (grad_near_w, grad_near_x), (grad_far_w, grad_far_x)
        steps = range(0, patches.shape[1], 256)
        some, others = steps[: len(steps) // 2], steps[len(steps) // 2 :]
        normed = (after(normed_w, go), normed_x)
        grad_w_up, grad_bias_up = weight_grad_up("wgrad_up_1", normed, nears, fars, me, units, some, None)
        came = along_gy(go, 1).astype(f32)
        grad_sums_w = keep + came[:n]
        gain = gain + (came[n : n + 1] + came[n + 8 : n + 9])
        keep, go = down_product("mlp_x", near_x, after(far_x, grad_bias_up), late_down, me)
        sums_x = pair_sum(keep, go)
        grad_held, _ = from_neighbour(grad_sums_x)
        normed = (after(normed_w, go, grad_sums_w, sums_x, *grad_held), normed_x)
        grad_w_up = weight_grad_up("wgrad_up_2", normed, nears, fars, me, units, others, grad_w_up)[0]
        held, _ = from_neighbour(sums_x, None, grad_w_up)
        keep, go = down_product("mlp_w", near_w, after(far_w, grad_w_up), late_down, me)
        sums_w = pair_sum(keep, go)
        far_w = after(far_w, go, sums_w)
        grad_w_down = weight_grad_down("wgrad_far", (far_w, far_x), (cot_w, cot_x), me, (1, 3), shard, units, down)
        grad_far, _ = from_far(grad_held)
        came, gain = swap(grad_sums_w[rows:], 2, gain)
        grad_normed = grad_sums_w[:rows] + after(came, go) + grad_far
        scaled = grad_normed * norm_gain
        sums = jnp.stack([jnp.sum(scaled, axis=1), jnp.sum(scaled * standard, axis=1)])
        sums = sums + along_gx(sums, 1)
        mlp_home = sums_w[:rows] + after(along_gy(sums_w[rows:].astype(bf16), 2), grad_w_down).astype(f32)
        held = [after(h, grad_w_up) for h in held]
        mlp_out = (mlp_home + from_far(held)[0] + bias_down).astype(bf16)
        for step in bits(chips)[1:]:
            gain = gain + after(along_gy(gain, 2 * step), grad_w_down)
        grad_gain = gain[0] / norm_gain

        grad_bias_down = jnp.sum(cot_w.astype(f32), axis=0) + jnp.sum(cot_x.astype(f32), axis=0)

        sums = plane_sum(sums, 2)
        first_mean = (sums[0] / D)[:, None]
        second_mean = (sums[1] / D)[:, None]
        grad_patches = (inv_std * (scaled - first_mean - standard * second_mean)).astype(bf16)
        return mlp_out, grad_patches, grad_gain, grad_w_up, grad_bias_up[0], grad_w_down, grad_bias_down

    in_specs = (
        P("gy", "gx"),
        P("gx"),
        P("gx", "gy"),
        P("gy"),
        P("gy", "gx"),
        P("gx"),
        P("gy", "gx"),
    )
    out_specs = (
        P("gy", "gx"),
        P("gy", "gx"),
        P("gx"),
        P("gx", "gy"),
        P("gy"),
        P("gy", "gx"),
        P("gx"),
    )
    return jax.shard_map(shards, mesh=mesh, in_specs=in_specs, out_specs=out_specs, check_vma=False)
```
